256 devices in a mesh: replica: 16 (over x, z_lo), pipe: 2 (over core), tensor: 8 (over y, z_hi).
Axes of the slice: x: 4, y: 4, z: 8 (z_hi: 2, z_lo: 4; z = z_hi * 4 + z_lo), core: 2. Of those that a mesh axis runs over, the one named last changes fastest.
Arguments:
- patches: bfloat16 [192, 4, 32, 1280], P('replica', 'pipe', None, 'tensor'), may hold values from -6 to 6
- tile_counts: int32 [192], replicated, may hold values from 1 to 4
- ln_gain: float32 [1280], replicated, may hold values from 0.1 to 1.9
- enc_qkv: bfloat16 [1280, 3, 1280], P(None, None, 'tensor'), may hold values from -0.15625 to 0.15625
- enc_out_w: bfloat16 [1280, 1280], P('tensor'), may hold values from -0.15625 to 0.15625
- proj_w: bfloat16 [1280, 8192], P(None, 'tensor'), may hold values from -0.15625 to 0.15625
- cross_kv_w: bfloat16 [8192, 2, 1024], P('tensor'), may hold values from -0.09375 to 0.09375
- k_gain: float32 [128], replicated, may hold values from 0.1 to 1.9
- plan: int32 [192, 1], replicated, may hold values from 0 to 15; in each aligned block of 12 rows (0 to 11, 12 to 23, ...) at most 2 rows name the same one
- row_pick: int32 [1024], P(('replica', 'pipe')), may hold values from 0 to 4095
- q_cross: bfloat16 [2, 1024, 8192], P(None, ('replica', 'pipe'), 'tensor'), may hold values from -6 to 6
- q_self: bfloat16 [2, 1024, 8192], P(None, ('replica', 'pipe'), 'tensor'), may hold values from -6 to 6
- cache_kv: bfloat16 [1024, 32, 2, 1024], P(('replica', 'pipe'), None, None, 'tensor'), may hold values from -6 to 6
- new_kv: bfloat16 [2, 1024, 2, 1024], P(None, ('replica', 'pipe'), None, 'tensor'), may hold values from -6 to 6
- kv_len: int32 [1024], P(('replica', 'pipe')), may hold values from 1 to 32
Outputs:
- cross_out: bfloat16 [2, 1024, 8192], P(None, ('replica', 'pipe'), 'tensor')
- self_out: bfloat16 [2, 1024, 8192], P(None, ('replica', 'pipe'), 'tensor')
The draws below stay inside these ranges and needn't reach their ends.
Inputs may be any that keep to these rules, and one draw needn't show every extreme that they name: `plan`: among the 12 images g * 12 to (g + 1) * 12 - 1 of one encoder group at most 2 have one replica, exactly 2 in some group; every replica is named by some image.
All inputs are finite; a program needn't handle non-finite values.
Results may differ from the reference program's by a relative error of at most 0.03.
Values may be sent and summed in bfloat16 or wider, within the bound.
No kernel may reach another device: no remote copies, remote signals or barrier semaphores. Data moves between devices by JAX's collectives and lax.ppermute only.
A program may use at most 128 MiB of HBM per device.

```python
import math
import jax
import jax.numpy as jnp
import numpy as np
from jax import lax

DM = 8192
HEADS = 64
KV_HEADS = 8
HD = 128
ENC_W = 1280
ENC_HEADS = 16
TILES = 4
TT = 32
IMGS_REP = 12
CAP = 2
ROWS_DEV = 32
STEPS = 2
LMAX = 32
NIMG = 192
DEC = 1024
N_REPLICA = 16
N_PIPE = 2


def set_ends(values, key, least, high):
    longest = values.shape.index(max(values.shape))
    spots = []
    for shift in (0, 1):
        where = [jax.random.randint(jax.random.fold_in(key, axis), (), 0, length) for axis, length in enumerate(values.shape)]
        where[longest] = (where[longest] + shift) % values.shape[longest]
        spots.append(tuple(where))
    return values.at[spots[0]].set(least).at[spots[1]].set(high)


def with_spikes(entries, stream_key, source, target, shards_of, factor):
    def block_of(position):
        return (jnp.arange(entries.shape[position]) // (entries.shape[position] // shards_of)).reshape((-1,) + (1,) * (entries.ndim - 1 - position))

    first = jax.random.permutation(stream_key, shards_of)[block_of(target)]
    second = (block_of(target) + shards_of // 2) % shards_of
    return jnp.where((block_of(source) == first) | (block_of(source) == second), factor * entries, entries)


def level_of(key, dims, cuts, least, largest):
    level, own = 1.0, jax.random.fold_in(key, 6)
    for position, parts in cuts:
        steps = jnp.exp(jax.random.uniform(jax.random.fold_in(own, position), (parts,), jnp.float32, least / len(cuts), largest / len(cuts)))
        level = level * jnp.repeat(steps, dims[position] // parts).reshape([-1 if axis == position else 1 for axis in range(len(dims))])
    return level


def routed_block(rng, own, number, rows, count, top, bound, skew):
    ranking = jax.random.permutation(rng, count)
    crowded, usual = load_shares(count, rows * top, bound, skew, True), load_shares(count, rows * top, bound, skew, False)
    places = jnp.arange(count)

    def named(sizes, offset_by):
        used = int((sizes > 0).sum())
        fixed = max(1, used // 4)
        shifted = fixed + (places - fixed + offset_by * (used - fixed)) % max(1, count - fixed)
        return jnp.zeros((count,), jnp.int32).at[ranking[jnp.where(places < fixed, places, shifted)]].set(jnp.asarray(sizes, jnp.int32))

    sizes = jnp.where(number % 4 == 0, named(crowded, number // 4), named(usual, number - number // 4 - 1))
    mixed = jax.random.permutation(jax.random.fold_in(own, 3), count)
    donor, sink = mixed[0:count // 2 * 2:2], mixed[1:count // 2 * 2:2]
    slack = jnp.minimum(sizes[donor] - 1, bound - sizes[sink]) // 2
    slack = jnp.where((donor == ranking[0]) | (sink == ranking[0]) | (sizes[sink] == 0), 0, jnp.maximum(slack, 0))
    shifted = jax.random.randint(jax.random.fold_in(own, 4), (count // 2,), 0, 1 << 20) % (slack + 1)
    sizes = sizes.at[donor].add(-shifted).at[sink].add(shifted)
    labels = jnp.searchsorted(jnp.cumsum(sizes), jnp.arange(rows * top), side="right").astype(jnp.int32)
    listing = labels.reshape(top, rows).T
    listing = listing[jax.random.permutation(jax.random.fold_in(own, 1), rows)]
    offset_by = jax.random.randint(jax.random.fold_in(own, 2), (rows, 1), 0, top)
    return jnp.take_along_axis(listing, (jnp.arange(top)[None, :] + offset_by) % top, axis=1)


def load_shares(number_of, total, limit, slope, full):
    weights = [(1 << 20) // math.isqrt(grade ** slope) + 1 for grade in range(1, number_of + 1)]
    largest = limit if full else min(limit, max(-(-total // number_of), total * weights[0] // sum(weights)))
    least = 1 if total - largest >= number_of - 1 else 0
    holding, rest = [largest] + [least] * (number_of - 1), total - largest - least * (number_of - 1)
    while rest > 0:
        candidates = [i for i in range(1, number_of) if holding[i] < largest] or [i for i in range(1, number_of) if holding[i] < limit]
        pool, budget = sum([weights[i] for i in candidates]), rest
        for i in candidates:
            extra = min(limit - holding[i], max(1, budget * weights[i] // pool), rest)
            holding[i] = holding[i] + extra
            rest = rest - extra
    return np.array(holding)


def noise(stream_key, dims, deviation, limit, cuts=(), kind=jnp.bfloat16):
    values = deviation * jax.random.normal(stream_key, dims, jnp.float32)
    if cuts:
        values = values * level_of(stream_key, dims, cuts, -0.22, 0.18)
    return jnp.clip(values, -limit, limit).astype(kind)


def heavy_noise(stream_key, shape, deviation, most, cuts, heavy, kind=jnp.bfloat16):
    values = deviation * jax.random.normal(stream_key, shape, jnp.float32)
    if cuts:
        values = values * level_of(stream_key, shape, cuts, -0.22, 0.18)
    return jnp.clip(with_spikes(values, jax.random.fold_in(stream_key, 3), *heavy), -most, most).astype(kind)


def setup_inputs(seed: int = 0) -> dict:
    key_of = jax.random.split(jax.random.key(seed), 16)
    patches = noise(key_of[0], (NIMG, TILES, TT, ENC_W), 1.0, 6.0, ((0, 16), (1, 2), (3, 8)))
    tile_counts = set_ends(jax.random.randint(key_of[1], (NIMG,), 1, TILES + 1), jax.random.fold_in(key_of[1], 1), 1, TILES).astype(jnp.int32)
    ln_gain = jnp.clip(1.0 + 0.18 * jax.random.normal(key_of[2], (ENC_W,), jnp.float32), 0.1, 1.9)
    enc_qkv = noise(key_of[3], (ENC_W, 3, ENC_W), ENC_W ** -0.5, 0.15625, ((2, 8),))
    enc_out_w = noise(key_of[4], (ENC_W, ENC_W), ENC_W ** -0.5, 0.15625, ((0, 8),))
    proj_w = noise(key_of[5], (ENC_W, DM), ENC_W ** -0.5, 0.15625, ((1, 8),))
    cross_kv_w = heavy_noise(key_of[6], (DM, 2, KV_HEADS * HD), DM ** -0.5, 0.09375, ((0, 8),), (0, 2, 8, 2.0))
    k_gain = jnp.clip(1.0 + 0.18 * jax.random.normal(key_of[7], (HD,), jnp.float32), 0.1, 1.9)
    plan_keys = jax.random.split(jax.random.fold_in(key_of[8], 1), NIMG // IMGS_REP)
    plan_turns = jax.random.permutation(jax.random.fold_in(key_of[8], 3), NIMG // IMGS_REP)
    plan = jax.vmap(lambda own, number: routed_block(jax.random.fold_in(key_of[8], 2), own, number, IMGS_REP, N_REPLICA, 1, CAP, 2))(plan_keys, plan_turns).reshape((NIMG, 1))
    row_pick = set_ends(jax.random.randint(key_of[9], (DEC,), 0, 4096), jax.random.fold_in(key_of[9], 1), 0, 4095).astype(jnp.int32)
    q_cross = noise(key_of[10], (STEPS, DEC, HEADS * HD), 1.0, 6.0, ((1, 32), (2, 8)))
    q_self = noise(key_of[11], (STEPS, DEC, HEADS * HD), 1.0, 6.0, ((1, 32), (2, 8)))
    cache_kv = noise(key_of[12], (DEC, LMAX, 2, KV_HEADS * HD), 1.0, 6.0, ((0, 32), (3, 8)))
    new_kv = noise(key_of[13], (STEPS, DEC, 2, KV_HEADS * HD), 1.0, 6.0, ((1, 32), (3, 8)))
    kv_len = set_ends(jax.random.randint(key_of[14], (DEC,), 1, LMAX + 1), jax.random.fold_in(key_of[14], 1), 1, LMAX).astype(jnp.int32)
    return {"patches": patches, "tile_counts": tile_counts, "ln_gain": ln_gain, "enc_qkv": enc_qkv, "enc_out_w": enc_out_w, "proj_w": proj_w, "cross_kv_w": cross_kv_w, "k_gain": k_gain, "plan": plan, "row_pick": row_pick, "q_cross": q_cross, "q_self": q_self, "cache_kv": cache_kv, "new_kv": new_kv, "kv_len": kv_len}


def norm_rows(values, gain):
    middle = lax.optimization_barrier(jnp.mean(values, -1, keepdims=True))
    centred = values - middle
    spread = lax.optimization_barrier(jnp.mean(centred * centred, -1, keepdims=True))
    return centred * lax.rsqrt(spread + 1e-06) * gain

def attend(query, keys, values, valid):
    scores = jnp.einsum('bkgd,btkd->bkgt', query.astype(jnp.float32), keys.astype(jnp.float32)) * query.shape[-1] ** (-0.5)
    scores = jnp.where(valid[:, None, None, :], scores, -1e+30)
    highest = lax.optimization_barrier(jnp.max(scores, -1, keepdims=True))
    weights = jnp.exp(scores - highest)
    probs = (weights / lax.optimization_barrier(jnp.sum(weights, -1, keepdims=True))).astype(jnp.bfloat16)
    mixed = jnp.einsum('bkgt,btkd->bkgd', probs.astype(jnp.float32), values.astype(jnp.float32))
    return mixed.astype(jnp.bfloat16)

def reference(patches, tile_counts, ln_gain, enc_qkv, enc_out_w, proj_w, cross_kv_w, k_gain, plan, row_pick, q_cross, q_self, cache_kv, new_kv, kv_len):
    head_dim = ENC_W // ENC_HEADS
    key_rows = TILES * TT

    def encode(pair):
        image, count = pair
        rows = image.astype(jnp.float32).reshape(key_rows, ENC_W)
        normed = norm_rows(rows, ln_gain).astype(jnp.bfloat16)
        projected = jnp.dot(normed, enc_qkv.reshape(ENC_W, 3 * ENC_W), preferred_element_type=jnp.float32)
        projected = projected.astype(jnp.bfloat16).reshape(key_rows, 3, ENC_HEADS, head_dim)
        valid = jnp.arange(key_rows) // TT < count
        scores = jnp.einsum('qhd,khd->hqk', projected[:, 0].astype(jnp.float32), projected[:, 1].astype(jnp.float32)) * head_dim ** (-0.5)
        scores = jnp.where(valid[None, None, :], scores, -1e+30)
        highest = lax.optimization_barrier(jnp.max(scores, -1, keepdims=True))
        weights = jnp.exp(scores - highest)
        probs = (weights / lax.optimization_barrier(jnp.sum(weights, -1, keepdims=True))).astype(jnp.bfloat16)
        mixed = jnp.einsum('hqk,khd->qhd', probs.astype(jnp.float32), projected[:, 2].astype(jnp.float32))
        mixed = mixed.astype(jnp.bfloat16).reshape(key_rows, ENC_W)
        encoded = (rows + jnp.dot(mixed, enc_out_w, preferred_element_type=jnp.float32)).astype(jnp.bfloat16)
        vision = jnp.dot(encoded, proj_w, preferred_element_type=jnp.float32).astype(jnp.bfloat16)
        summed = jnp.dot(vision, cross_kv_w.reshape(DM, 2 * KV_HEADS * HD), preferred_element_type=jnp.float32)
        summed = summed.reshape(key_rows, 2, KV_HEADS, HD)
        key_heads = summed[:, 0]
        key_heads = key_heads * lax.rsqrt(lax.optimization_barrier(jnp.mean(key_heads * key_heads, -1, keepdims=True)) + 1e-05) * k_gain
        return jnp.stack([key_heads, summed[:, 1]], 1).astype(jnp.bfloat16)
    memory = lax.map(encode, (patches, tile_counts))
    destination = plan[:, 0]
    row_group = jnp.arange(DEC) // (ROWS_DEV * N_PIPE)
    mine = (destination[None, :] == row_group[:, None]).astype(jnp.int32)
    count = lax.optimization_barrier(jnp.sum(mine, 1))
    before = jnp.cumsum(mine, 1) - mine
    wanted = row_pick % count
    hit = (mine == 1) & (before == wanted[:, None])
    chosen = lax.optimization_barrier(jnp.sum(jnp.where(hit, jnp.arange(NIMG, dtype=jnp.int32)[None, :], 0), 1)).astype(jnp.int32)
    chosen_counts = tile_counts[chosen]
    blocks = DEC // ROWS_DEV
    group_size = HEADS // KV_HEADS

    def split_rows(array):
        shaped = array.reshape((array.shape[0], blocks, ROWS_DEV) + array.shape[2:])
        return jnp.moveaxis(shaped, 1, 0)

    def decode(pieces):
        cross_q, self_q, cache, fresh_all, lengths, picks, counts_here = pieces
        memory_rows = memory[picks]
        valid_cross = (jnp.arange(key_rows) // TT)[None, :] < counts_here[:, None]
        cache_valid = jnp.arange(LMAX)[None, :] < lengths[:, None]
        cross_list = []
        self_list = []
        for step_index in range(STEPS):
            query = cross_q[step_index].reshape(ROWS_DEV, KV_HEADS, group_size, HD)
            result = attend(query, memory_rows[:, :, 0], memory_rows[:, :, 1], valid_cross)
            cross_list.append(result.reshape(ROWS_DEV, HEADS * HD))
            fresh = jnp.moveaxis(fresh_all[:step_index + 1], 0, 1)
            joined = jnp.concatenate([cache, fresh], 1).reshape(ROWS_DEV, LMAX + step_index + 1, 2, KV_HEADS, HD)
            valid_self = jnp.concatenate([cache_valid, jnp.ones((ROWS_DEV, step_index + 1), bool)], 1)
            query = self_q[step_index].reshape(ROWS_DEV, KV_HEADS, group_size, HD)
            result = attend(query, joined[:, :, 0], joined[:, :, 1], valid_self)
            self_list.append(result.reshape(ROWS_DEV, HEADS * HD))
        return (jnp.stack(cross_list), jnp.stack(self_list))
    pieces = (split_rows(q_cross), split_rows(q_self), cache_kv.reshape((blocks, ROWS_DEV) + cache_kv.shape[1:]), split_rows(new_kv), kv_len.reshape(blocks, ROWS_DEV), chosen.reshape(blocks, ROWS_DEV), chosen_counts.reshape(blocks, ROWS_DEV))
    cross_blocks, self_blocks = lax.map(decode, pieces)
    cross_out = jnp.moveaxis(cross_blocks, 0, 1).reshape(STEPS, DEC, HEADS * HD)
    self_out = jnp.moveaxis(self_blocks, 0, 1).reshape(STEPS, DEC, HEADS * HD)
    return (cross_out, self_out)
```

```python
import functools

import jax
import jax.numpy as jnp
from jax import lax
from jax.experimental import pallas as pl
from jax.experimental.pallas import tpu as pltpu
from jax.sharding import PartitionSpec as P

HEADS = 64
KV_HEADS = 8
HD = 128
ENC_W = 1280
ENC_HEADS = 16
CAP = 2
STEPS = 2
LMAX = 32
TT = 32
LIMIT = 48 * 1024 * 1024
BF = jnp.bfloat16
F32 = jnp.float32

VMEM = pl.BlockSpec(memory_space=pltpu.VMEM)
SMEM = pl.BlockSpec(memory_space=pltpu.SMEM)
ANY = pl.BlockSpec(memory_space=pl.ANY)


def call(kernel, outs, in_specs, scratch, flops, moved, name):
    return pl.pallas_call(
        kernel,
        out_shape=outs,
        in_specs=in_specs,
        out_specs=jax.tree.map(lambda _: VMEM, outs),
        scratch_shapes=scratch,
        compiler_params=pltpu.CompilerParams(vmem_limit_bytes=LIMIT),
        cost_estimate=pl.CostEstimate(flops=flops, bytes_accessed=moved, transcendentals=0),
        name=name,
    )


def shape_of(shape, dtype):
    return jax.ShapeDtypeStruct(shape, dtype)


def dot(a, b, dims):
    return lax.dot_general(a, b, (dims, ((), ())), preferred_element_type=F32)


def turn_kernel(x_ref, out_ref):
    width = x_ref.shape[1]
    row = lax.broadcasted_iota(jnp.int32, (width, width), 0)
    col = lax.broadcasted_iota(jnp.int32, (width, width), 1)
    eye = jnp.where(row == col, 1.0, 0.0).astype(BF)
    out_ref[...] = dot(eye, x_ref[...], ((1,), (1,))).astype(BF)


def qkv_kernel(off_ref, *refs):
    shards = refs[:8]
    w_ref, gain_ref, q_ref, kv_ref, normed = refs[8:]
    part = shards[0].shape[0]
    width = part * 8
    total = jnp.zeros((1, shards[0].shape[1]), F32)
    for s in shards:
        total += jnp.sum(s[...].astype(F32), 0, keepdims=True)
    mean = total / width
    total = jnp.zeros_like(mean)
    for s in shards:
        c = s[...].astype(F32) - mean
        total += jnp.sum(c * c, 0, keepdims=True)
    scale = lax.rsqrt(total / width + 1e-06)
    for i, s in enumerate(shards):
        at = pl.ds(pl.multiple_of(off_ref[i] * part, 16), part)
        c = s[...].astype(F32) - mean
        normed[at, :] = (c * scale * gain_ref[at, :]).astype(BF)
    out = jnp.dot(w_ref[...], normed[...], preferred_element_type=F32).astype(BF)
    q_ref[...] = out[:part]
    kv_ref[...] = out[part:]


def attend_kernel(count_ref, pipe_ref, q_ref, own_ref, other_ref, out_ref):
    part, rows = q_ref.shape
    heads = 2
    hd = part // heads
    pipe = pipe_ref[0]
    key = lax.broadcasted_iota(jnp.int32, (256, 1), 0)
    from_other = key // 128
    key_image = (key % 128) // 64
    tile = 2 * jnp.where(from_other == 1, 1 - pipe, pipe) + (key % 64) // TT
    lane_image = lax.broadcasted_iota(jnp.int32, (1, 128), 1) // 64
    for j in range(rows // 128):
        lanes = slice(j * 128, (j + 1) * 128)
        count = jnp.where(lane_image == 0, count_ref[2 * j], count_ref[2 * j + 1])
        valid = (key_image == lane_image) & (tile < count)
        for h in range(heads):
            k_at = slice(h * hd, (h + 1) * hd)
            v_at = slice(part + h * hd, part + (h + 1) * hd)
            keys = jnp.concatenate([own_ref[k_at, lanes], other_ref[k_at, lanes]], 1)
            values = jnp.concatenate([own_ref[v_at, lanes], other_ref[v_at, lanes]], 1)
            scores = dot(keys, q_ref[k_at, lanes], ((0,), (0,))) * hd ** (-0.5)
            scores = jnp.where(valid, scores, -1e30)
            weights = jnp.exp(scores - jnp.max(scores, 0, keepdims=True))
            probs = (weights / jnp.sum(weights, 0, keepdims=True)).astype(BF)
            out_ref[k_at, lanes] = jnp.dot(values, probs, preferred_element_type=F32).astype(BF)


def fill(off_ref, shards, full, sems):
    part = shards[0].shape[0]
    copies = []
    for i, s in enumerate(shards):
        at = pl.ds(pl.multiple_of(off_ref[i] * part, 16), part)
        copies.append(pltpu.make_async_copy(s, full.at[at, :], sems.at[i]))
    for c in copies:
        c.start()
    for c in copies:
        c.wait()


def own_term_kernel(off_ref, *refs):
    shards = refs[:8]
    w_ref, out_ref, full, sems = refs[8:]
    fill(off_ref, shards, full, sems)
    out_ref[...] = jnp.dot(w_ref[...], full[...], preferred_element_type=F32)


def memory_kernel(off_ref, pick_ref, *refs):
    shards = refs[:8]
    w_ref, own_ref, gain_ref, out_ref, full, rows_ref, sems = refs[8:]
    fill(off_ref, shards, full, sems)
    kv = jnp.dot(w_ref[...], full[...], preferred_element_type=F32) + own_ref[...]
    keys = kv[:HD]
    keys = keys * lax.rsqrt(jnp.mean(keys * keys, 0, keepdims=True) + 1e-05) * gain_ref[...]
    rows_ref[:, :HD] = jnp.transpose(keys).astype(BF)
    rows_ref[:, HD:] = jnp.transpose(kv[HD:]).astype(BF)
    for i in range(out_ref.shape[0] // 64):
        at = pl.ds(pl.multiple_of(pick_ref[i] * 64, 64), 64)
        out_ref[i * 64 : (i + 1) * 64, :] = rows_ref[at, :]


def finish(score_ref, mixed_ref, valid, out_ref):
    rows = out_ref.shape[1]
    scores = jnp.where(valid, score_ref[...] * HD ** (-0.5), -1e30)
    weights = jnp.exp(scores - jnp.max(scores, 1, keepdims=True))
    return (weights / jnp.sum(weights, 1, keepdims=True)).astype(BF)


def spread(mixed_ref, out_ref):
    group = out_ref.shape[2] // HD
    for s in range(STEPS):
        for h in range(group):
            out_ref[s, :, h * HD : (h + 1) * HD] = mixed_ref[:, s * group + h, :].astype(BF)


def cross_kernel(slot_ref, pipe_ref, count_ref, q_ref, own_ref, other_ref, out_ref, score_ref, prob_ref, mixed_ref):
    rows, per = q_ref.shape[0], q_ref.shape[1]
    pipe = pipe_ref[0]
    for b in range(rows):
        at = pl.ds(pl.multiple_of(slot_ref[b] * 64, 64), 64)
        keys = jnp.concatenate([own_ref[at, :HD], other_ref[at, :HD]], 0)
        score_ref[b * per : (b + 1) * per, :] = dot(q_ref[b], keys, ((1,), (1,)))
    lane = lax.broadcasted_iota(jnp.int32, (1, 128), 1)
    tile = 2 * jnp.where(lane >= 64, 1 - pipe, pipe) + (lane % 64) // TT
    prob_ref[...] = finish(score_ref, mixed_ref, tile < count_ref[...], out_ref)
    for b in range(rows):
        at = pl.ds(pl.multiple_of(slot_ref[b] * 64, 64), 64)
        values = jnp.concatenate([own_ref[at, HD:], other_ref[at, HD:]], 0)
        mixed_ref[b] = jnp.dot(
            prob_ref[b * per : (b + 1) * per, :], values, preferred_element_type=F32
        )
    spread(mixed_ref, out_ref)


def self_kernel(len_ref, q_ref, kv_ref, out_ref, score_ref, prob_ref, mixed_ref):
    rows, per = q_ref.shape[0], q_ref.shape[1]
    for b in range(rows):
        score_ref[b * per : (b + 1) * per, :] = dot(q_ref[b], kv_ref[b, :, :HD], ((1,), (1,)))
    spots = kv_ref.shape[1]
    lane = lax.broadcasted_iota(jnp.int32, (1, spots), 1)
    step = (lax.broadcasted_iota(jnp.int32, (rows * per, 1), 0) % per) // (per // STEPS)
    valid = (lane < len_ref[...]) | ((lane >= LMAX) & (lane <= LMAX + step))
    prob_ref[...] = finish(score_ref, mixed_ref, valid, out_ref)
    for b in range(rows):
        mixed_ref[b] = jnp.dot(
            prob_ref[b * per : (b + 1) * per, :], kv_ref[b, :, HD:], preferred_element_type=F32
        )
    spread(mixed_ref, out_ref)


ZX = [(t, t ^ 1) for t in range(8)]


def y_perm(d):
    return [(t, (t + 2 * d) % 8) for t in range(8)]


def gather8(s):
    p1, p2, p3 = y_perm(1), y_perm(2), y_perm(3)
    z = lax.ppermute(s, "tensor", ZX)
    a, b, c = (lax.ppermute(s, "tensor", p) for p in (p1, p3, p2))
    za, zb, zc = (lax.ppermute(z, "tensor", p) for p in (p1, p3, p2))
    return (s, z, a, b, c, za, zb, zc)


def gather_order(t):
    a, b, c = (t + 6) % 8, (t + 2) % 8, (t + 4) % 8
    return jnp.stack([t, t ^ 1, a, b, c, a ^ 1, b ^ 1, c ^ 1]).astype(jnp.int32)


def fold_weights(enc_out_w, proj_w, cross_kv_w, u, tensor):
    y, zh = tensor // 2, tensor % 2
    per = ENC_W // 32
    few = per // 8
    mine = lax.dynamic_slice_in_dim(enc_out_w, u * few, few)
    other = lax.ppermute(mine, "tensor", ZX)
    pair = jnp.where(zh == 0, jnp.stack([mine, other]), jnp.stack([other, mine]))
    rel = jnp.stack([pair] + [lax.ppermute(pair, "tensor", y_perm(d)) for d in (1, 2, 3)])
    whole = jnp.take(rel, (y - jnp.arange(4)) % 4, axis=0).reshape(per, ENC_W)
    folded = jnp.dot(whole, proj_w, preferred_element_type=F32).astype(BF)
    left = jnp.concatenate([lax.dynamic_slice_in_dim(proj_w, u * per, per), folded], 0)
    part = jnp.einsum(
        "rk,kcn->crn", left, cross_kv_w, preferred_element_type=F32
    ).astype(BF)
    part = part.reshape(2, 2 * per, 4, 2, HD).transpose(3, 2, 1, 0, 4).reshape(2, 4, 2 * per, 2 * HD)
    keep = lax.dynamic_index_in_dim(part, zh, 0, keepdims=False)
    send = lax.dynamic_index_in_dim(part, 1 - zh, 0, keepdims=False)
    half = keep.astype(F32) + lax.ppermute(send, "tensor", ZX).astype(F32)
    total = lax.dynamic_index_in_dim(half, y, 0, keepdims=False)
    half = half.astype(BF)
    for d in (1, 2, 3):
        block = lax.dynamic_index_in_dim(half, (y + d) % 4, 0, keepdims=False)
        total = total + lax.ppermute(block, "tensor", y_perm(d)).astype(F32)
    return total.astype(BF)


def spread_weights(piece, replica, pipe):
    x, zl = replica // 4, replica % 4
    zs = [piece] + [
        lax.ppermute(piece, "replica", [(r, r // 4 * 4 + (r + d) % 4) for r in range(16)])
        for d in (1, 2, 3)
    ]
    line = jnp.take(jnp.stack(zs), (zl - jnp.arange(4)) % 4, axis=0)
    xs = [line] + [
        lax.ppermute(line, "replica", [(r, (r + 4 * d) % 16) for r in range(16)])
        for d in (1, 2, 3)
    ]
    plane = jnp.take(jnp.stack(xs), (x - jnp.arange(4)) % 4, axis=0)
    other = lax.ppermute(plane, "pipe", [(0, 1), (1, 0)])
    both = jnp.where(pipe == 0, jnp.stack([plane, other], 2), jnp.stack([other, plane], 2))
    per = piece.shape[0] // 2
    both = both.reshape(32, 2, per, 2 * HD)
    first = both[:, 0].reshape(ENC_W, 2 * HD)
    second = both[:, 1].reshape(32, 8, per // 8, 2 * HD).transpose(1, 0, 2, 3).reshape(ENC_W, 2 * HD)
    return first.T, second.T


def shards(
    patches,
    tile_counts,
    ln_gain,
    enc_qkv,
    enc_out_w,
    proj_w,
    cross_kv_w,
    k_gain,
    plan,
    row_pick,
    q_cross,
    q_self,
    cache_kv,
    new_kv,
    kv_len,
):
    replicas = 16
    group = lax.axis_index("replica")
    pipe = lax.axis_index("pipe")
    tensor = lax.axis_index("tensor")
    images, held, tile_rows, part = patches.shape
    rows = images * held * tile_rows
    order = gather_order(tensor)
    pipe_at = pipe.reshape(1).astype(jnp.int32)

    turned = call(
        turn_kernel, shape_of((part, rows), BF), [VMEM], [], 2 * rows * part * part, 4 * rows * part, "turn"
    )(patches.reshape(rows, part))
    xs = gather8(turned)

    u = group * 2 + pipe
    piece = fold_weights(enc_out_w, proj_w, cross_kv_w, u, tensor)
    w_own, w_mixed = spread_weights(piece, group, pipe)

    rows_here = row_pick.shape[0]
    steps_heads = q_self.shape[0] * q_self.shape[2] // HD

    def heads_of(q):
        return q.reshape(STEPS, rows_here, -1, HD).transpose(1, 0, 2, 3).reshape(rows_here, steps_heads, HD)

    spots = 48
    joined = jnp.concatenate(
        [
            cache_kv.reshape(rows_here, LMAX, 2 * HD),
            jnp.moveaxis(new_kv, 0, 1).reshape(rows_here, STEPS, 2 * HD),
            jnp.zeros((rows_here, spots - LMAX - STEPS, 2 * HD), BF),
        ],
        1,
    )

    def per_head(values):
        return jnp.repeat(values.astype(jnp.int32), steps_heads).reshape(rows_here * steps_heads, 1)

    def scratch(n):
        return [
            pltpu.VMEM((rows_here * steps_heads, n), F32),
            pltpu.VMEM((rows_here * steps_heads, n), BF),
            pltpu.VMEM((rows_here, steps_heads, HD), F32),
        ]

    self_out = call(
        self_kernel,
        shape_of(q_self.shape, BF),
        [VMEM] * 3,
        scratch(spots),
        4 * rows_here * 16 * 128 * 128,
        4 * 1024 * 1024,
        "self_attend",
    )(per_head(kv_len), heads_of(q_self), joined)

    turned_w = enc_qkv.transpose(1, 2, 0).reshape(3 * part, ENC_W)
    q, kv = call(
        qkv_kernel,
        (shape_of((part, rows), BF), shape_of((2 * part, rows), BF)),
        [SMEM] + [VMEM] * 10,
        [pltpu.VMEM((ENC_W, rows), BF)],
        2 * rows * ENC_W * 3 * part,
        6 * 1024 * 1024,
        "qkv",
    )(order, *xs, turned_w, ln_gain.reshape(ENC_W, 1))
    kv_other = lax.ppermute(kv, "pipe", [(0, 1), (1, 0)])
    counts_local = lax.dynamic_slice_in_dim(tile_counts, group * images, images)
    mixed = call(
        attend_kernel,
        shape_of((part, rows), BF),
        [SMEM, SMEM, VMEM, VMEM, VMEM],
        [],
        4 * rows * 256 * part,
        2 * 1024 * 1024,
        "encoder_attend",
    )(counts_local, pipe_at, q, kv, kv_other)

    own_term = call(
        own_term_kernel,
        shape_of((2 * HD, rows), F32),
        [SMEM] + [ANY] * 8 + [VMEM],
        [pltpu.VMEM((ENC_W, rows), BF), pltpu.SemaphoreType.DMA((8,))],
        2 * rows * ENC_W * 2 * HD,
        4 * 1024 * 1024,
        "own_term",
    )(order, *xs, w_own)

    ms = gather8(mixed)

    destination = plan[:, 0]
    grouped = destination.reshape(replicas, images)
    earlier = jnp.arange(images)[:, None] < jnp.arange(images)[None, :]
    same_dest = grouped[:, :, None] == grouped[:, None, :]
    ranks = jnp.sum((same_dest & earlier[None]).astype(jnp.int32), 1)
    my_dest = lax.dynamic_index_in_dim(grouped, group, 0, keepdims=False)
    my_rank = lax.dynamic_index_in_dim(ranks, group, 0, keepdims=False)
    spot = my_dest * CAP + my_rank
    picks = jnp.sum(
        jnp.where(
            spot[None, :] == jnp.arange(replicas * CAP)[:, None],
            jnp.arange(images, dtype=jnp.int32)[None, :],
            0,
        ),
        1,
    ).astype(jnp.int32)
    mine = (destination == group).astype(jnp.int32)
    count = jnp.sum(mine)
    before = jnp.cumsum(mine) - mine
    wanted = row_pick % count
    hit = (mine[None, :] == 1) & (before[None, :] == wanted[:, None])
    every = jnp.arange(replicas * images, dtype=jnp.int32)
    slot_of = (every // images) * CAP + ranks.reshape(-1)
    slot_ids = jnp.sum(jnp.where(hit, slot_of[None, :], 0), 1).astype(jnp.int32)
    counts_rows = jnp.sum(jnp.where(hit, tile_counts[None, :], 0), 1).astype(jnp.int32)

    slots = call(
        memory_kernel,
        shape_of((replicas * CAP * held * tile_rows, 2 * HD), BF),
        [SMEM, SMEM] + [ANY] * 8 + [VMEM] * 3,
        [
            pltpu.VMEM((ENC_W, rows), BF),
            pltpu.VMEM((rows, 2 * HD), BF),
            pltpu.SemaphoreType.DMA((8,)),
        ],
        2 * rows * ENC_W * 2 * HD,
        4 * 1024 * 1024,
        "memory",
    )(order, picks, *ms, w_mixed, own_term, k_gain.reshape(HD, 1))
    arrived = lax.all_to_all(slots, "replica", split_axis=0, concat_axis=0, tiled=True)
    arrived_other = lax.ppermute(arrived, "pipe", [(0, 1), (1, 0)])

    cross_out = call(
        cross_kernel,
        shape_of(q_cross.shape, BF),
        [SMEM, SMEM] + [VMEM] * 4,
        scratch(128),
        4 * rows_here * 16 * 128 * 128,
        4 * 1024 * 1024,
        "cross_attend",
    )(slot_ids, pipe_at, per_head(counts_rows), heads_of(q_cross), arrived, arrived_other)
    return (cross_out, self_out)


def solution(mesh):
    in_specs = (
        P("replica", "pipe", None, "tensor"),
        P(),
        P(),
        P(None, None, "tensor"),
        P("tensor", None),
        P(None, "tensor"),
        P("tensor", None, None),
        P(),
        P(),
        P(("replica", "pipe")),
        P(None, ("replica", "pipe"), "tensor"),
        P(None, ("replica", "pipe"), "tensor"),
        P(("replica", "pipe"), None, None, "tensor"),
        P(None, ("replica", "pipe"), None, "tensor"),
        P(("replica", "pipe")),
    )
    out_specs = (P(None, ("replica", "pipe"), "tensor"), P(None, ("replica", "pipe"), "tensor"))
    return jax.shard_map(shards, mesh=mesh, in_specs=in_specs, out_specs=out_specs, check_vma=False)
```

```python
import functools

import jax
import jax.numpy as jnp
from jax import lax
from jax.experimental import pallas as pl
from jax.experimental.pallas import tpu as pltpu
from jax.sharding import PartitionSpec as P

HEADS = 64
KV_HEADS = 8
HD = 128
ENC_W = 1280
ENC_HEADS = 16
CAP = 2
STEPS = 2
LMAX = 32
TT = 32
LIMIT = 62 * 1024 * 1024
BF = jnp.bfloat16
F32 = jnp.float32

VMEM = pl.BlockSpec(memory_space=pltpu.VMEM)
SMEM = pl.BlockSpec(memory_space=pltpu.SMEM)
ANY = pl.BlockSpec(memory_space=pl.ANY)


def call(kernel, outs, in_specs, scratch, flops, moved, name):
    return pl.pallas_call(
        kernel,
        out_shape=outs,
        in_specs=in_specs,
        out_specs=jax.tree.map(lambda _: VMEM, outs),
        scratch_shapes=scratch,
        compiler_params=pltpu.CompilerParams(vmem_limit_bytes=LIMIT),
        cost_estimate=pl.CostEstimate(flops=flops, bytes_accessed=moved, transcendentals=0),
        name=name,
    )


def shape_of(shape, dtype):
    return jax.ShapeDtypeStruct(shape, dtype)


def dot(a, b, dims):
    return lax.dot_general(a, b, (dims, ((), ())), preferred_element_type=F32)


def turn_kernel(x_ref, out_ref):
    width = x_ref.shape[1]
    row = lax.broadcasted_iota(jnp.int32, (width, width), 0)
    col = lax.broadcasted_iota(jnp.int32, (width, width), 1)
    eye = jnp.where(row == col, 1.0, 0.0).astype(BF)
    out_ref[...] = dot(eye, x_ref[...], ((1,), (1,))).astype(BF)


def qkv_kernel(off_ref, *refs):
    shards = refs[:8]
    w_ref, gain_ref, q_ref, kv_ref, full, sems = refs[8:]
    part, rows = shards[0].shape
    width = part * 8
    fill(off_ref, shards, (full,), (sems,))
    cut = 256
    for j in range(rows // cut):
        lanes = slice(j * cut, (j + 1) * cut)
        base = full[0:1, lanes].astype(F32)
        total, squares = jnp.zeros((1, cut), F32), jnp.zeros((1, cut), F32)
        for i in range(8):
            c = full[i * part : (i + 1) * part, lanes].astype(F32) - base
            total += jnp.sum(c, 0, keepdims=True)
            squares += jnp.sum(c * c, 0, keepdims=True)
        shift = total / width
        mean = base + shift
        scale = lax.rsqrt(jnp.maximum(squares / width - shift * shift, 0.0) + 1e-06)
        for i in range(8):
            at = slice(i * part, (i + 1) * part)
            c = full[at, lanes].astype(F32) - mean
            full[at, lanes] = (c * scale * gain_ref[at, :]).astype(BF)
        out = jnp.dot(w_ref[...], full[:, lanes], preferred_element_type=F32).astype(BF)
        q_ref[:, lanes] = out[:part]
        kv_ref[:, lanes] = out[part:]


def attend_kernel(count_ref, pipe_ref, q_ref, own_ref, other_ref, out_ref):
    part, rows = q_ref.shape
    heads = 2
    hd = part // heads
    pipe = pipe_ref[0]
    key = lax.broadcasted_iota(jnp.int32, (256, 1), 0)
    from_other = key // 128
    key_image = (key % 128) // 64
    tile = 2 * jnp.where(from_other == 1, 1 - pipe, pipe) + (key % 64) // TT
    lane_image = lax.broadcasted_iota(jnp.int32, (1, 128), 1) // 64
    for j in range(rows // 128):
        lanes = slice(j * 128, (j + 1) * 128)
        count = jnp.where(lane_image == 0, count_ref[2 * j], count_ref[2 * j + 1])
        valid = (key_image == lane_image) & (tile < count)
        for h in range(heads):
            k_at = slice(h * hd, (h + 1) * hd)
            v_at = slice(part + h * hd, part + (h + 1) * hd)
            keys = jnp.concatenate([own_ref[k_at, lanes], other_ref[k_at, lanes]], 1)
            values = jnp.concatenate([own_ref[v_at, lanes], other_ref[v_at, lanes]], 1)
            scores = dot(keys, q_ref[k_at, lanes], ((0,), (0,))) * hd ** (-0.5)
            scores = jnp.where(valid, scores, -1e30)
            weights = jnp.exp(scores - jnp.max(scores, 0, keepdims=True))
            probs = (weights / jnp.sum(weights, 0, keepdims=True)).astype(BF)
            out_ref[k_at, lanes] = jnp.dot(values, probs, preferred_element_type=F32).astype(BF)


def fill(off_ref, shards, fulls, sems):
    part = shards[0].shape[0]
    copies = []
    for i, s in enumerate(shards):
        at = pl.ds(pl.multiple_of(off_ref[i % 8] * part, 16), part)
        copies.append(pltpu.make_async_copy(s, fulls[i // 8].at[at, :], sems[i // 8].at[i % 8]))
    for c in copies:
        c.start()
    for c in copies:
        c.wait()


def memory_kernel(off_ref, pick_ref, pipe_ref, *refs):
    xs, ms = refs[:8], refs[8:16]
    own_ref, other_ref, gain_ref, out_ref, x_ref, m_ref, rows_ref, x_sems, m_sems = refs[16:]
    fill(off_ref, xs + ms, (x_ref, m_ref), (x_sems, m_sems))
    half = own_ref.shape[0] // 2
    mine = pl.ds(pl.multiple_of(pipe_ref[0] * half, 128), half)
    rest = pl.ds(pl.multiple_of((1 - pipe_ref[0]) * half, 128), half)
    first = ((0,), (0,))
    kv = dot(own_ref[:half], x_ref[mine, :], first) + dot(other_ref[:half], x_ref[rest, :], first)
    kv += dot(own_ref[half:], m_ref[mine, :], first) + dot(other_ref[half:], m_ref[rest, :], first)
    keys = kv[:HD]
    keys = keys * lax.rsqrt(jnp.mean(keys * keys, 0, keepdims=True) + 1e-05) * gain_ref[...]
    rows_ref[:, :HD] = jnp.transpose(keys).astype(BF)
    rows_ref[:, HD:] = jnp.transpose(kv[HD:]).astype(BF)
    for i in range(out_ref.shape[0] // 64):
        at = pl.ds(pl.multiple_of(pick_ref[i] * 64, 64), 64)
        out_ref[i * 64 : (i + 1) * 64, :] = rows_ref[at, :]


def finish(score_ref, mixed_ref, valid, out_ref):
    rows = out_ref.shape[1]
    scores = jnp.where(valid, score_ref[...] * HD ** (-0.5), -1e30)
    weights = jnp.exp(scores - jnp.max(scores, 1, keepdims=True))
    return (weights / jnp.sum(weights, 1, keepdims=True)).astype(BF)


def spread(mixed_ref, out_ref):
    group = out_ref.shape[2] // HD
    for s in range(STEPS):
        for h in range(group):
            out_ref[s, :, h * HD : (h + 1) * HD] = mixed_ref[:, s * group + h, :].astype(BF)


def cross_kernel(slot_ref, pipe_ref, count_ref, q_ref, own_ref, other_ref, out_ref, score_ref, prob_ref, mixed_ref):
    rows, per = q_ref.shape[0], q_ref.shape[1]
    pipe = pipe_ref[0]
    for b in range(rows):
        at = pl.ds(pl.multiple_of(slot_ref[b] * 64, 64), 64)
        keys = jnp.concatenate([own_ref[at, :HD], other_ref[at, :HD]], 0)
        score_ref[b * per : (b + 1) * per, :] = dot(q_ref[b], keys, ((1,), (1,)))
    lane = lax.broadcasted_iota(jnp.int32, (1, 128), 1)
    tile = 2 * jnp.where(lane >= 64, 1 - pipe, pipe) + (lane % 64) // TT
    prob_ref[...] = finish(score_ref, mixed_ref, tile < count_ref[...], out_ref)
    for b in range(rows):
        at = pl.ds(pl.multiple_of(slot_ref[b] * 64, 64), 64)
        values = jnp.concatenate([own_ref[at, HD:], other_ref[at, HD:]], 0)
        mixed_ref[b] = jnp.dot(
            prob_ref[b * per : (b + 1) * per, :], values, preferred_element_type=F32
        )
    spread(mixed_ref, out_ref)


def self_kernel(len_ref, q_ref, kv_ref, out_ref, score_ref, prob_ref, mixed_ref):
    rows, per = q_ref.shape[0], q_ref.shape[1]
    for b in range(rows):
        score_ref[b * per : (b + 1) * per, :] = dot(q_ref[b], kv_ref[b, :, :HD], ((1,), (1,)))
    spots = kv_ref.shape[1]
    lane = lax.broadcasted_iota(jnp.int32, (1, spots), 1)
    step = (lax.broadcasted_iota(jnp.int32, (rows * per, 1), 0) % per) // (per // STEPS)
    valid = (lane < len_ref[...]) | ((lane >= LMAX) & (lane <= LMAX + step))
    prob_ref[...] = finish(score_ref, mixed_ref, valid, out_ref)
    for b in range(rows):
        mixed_ref[b] = jnp.dot(
            prob_ref[b * per : (b + 1) * per, :], kv_ref[b, :, HD:], preferred_element_type=F32
        )
    spread(mixed_ref, out_ref)


ZX = [(t, t ^ 1) for t in range(8)]


def y_perm(d):
    return [(t, (t + 2 * d) % 8) for t in range(8)]


def gather8(s, near=None):
    p1, p2, p3 = y_perm(1), y_perm(2), y_perm(3)
    z = lax.ppermute(s, "tensor", ZX)
    s = s if near is None else near
    a, b, c = (lax.ppermute(s, "tensor", p) for p in (p1, p3, p2))
    z = after(z, *((a, b, c) if near is None else ()))
    za, zb, zc = (lax.ppermute(z, "tensor", p) for p in (p1, p3, p2))
    return (s, z, a, b, c, za, zb, zc)


def gather_order(t):
    a, b, c = (t + 6) % 8, (t + 2) % 8, (t + 4) % 8
    return jnp.stack([t, t ^ 1, a, b, c, a ^ 1, b ^ 1, c ^ 1]).astype(jnp.int32)


def after(value, *others):
    return lax.optimization_barrier((value,) + others)[0]


def swap(values, axis, bit, size):
    return lax.ppermute(values, axis, [(i, i ^ bit) for i in range(size)])


def choose(flag, a, b):
    return jnp.where(flag, a, b)


def out_rows(enc_out_w, replica, pipe):
    per = ENC_W // 32
    pairs = []
    for r in range(16):
        for p in range(2):
            for t in range(8):
                part = p * 4 + r // 4
                near = t % 2 == part % 2
                source = t // 2 * 4 + (r % 4 if near else 3 - r % 4)
                core = 0 if near else 1
                pairs.append(((source * 2 + core) * 8 + part, (r * 2 + p) * 8 + t))
    block = jnp.where(pipe == 0, replica % 4, 3 - replica % 4)
    mine = lax.dynamic_slice_in_dim(enc_out_w, block * per, per)
    return lax.ppermute(mine, ("replica", "pipe", "tensor"), pairs)


def heads_kernel(part_ref, out_ref):
    for h in range(KV_HEADS):
        out_ref[h, :, :HD] = part_ref[0, :, h * HD : (h + 1) * HD]
        out_ref[h, :, HD:] = part_ref[1, :, h * HD : (h + 1) * HD]


def fold_weights(few, proj_w, cross_kv_w, replica, pipe, hold, late):
    per = ENC_W // 32
    folded = jnp.dot(few, proj_w, preferred_element_type=F32).astype(BF)
    left = lax.dynamic_slice_in_dim(proj_w, (pipe * 16 + replica) * per, per)
    left = after(jnp.concatenate([left, folded], 0), *hold)
    part = jnp.einsum("rk,kcn->crn", left, cross_kv_w, preferred_element_type=F32).astype(BF)
    blocks = call(
        heads_kernel,
        shape_of((KV_HEADS, 2 * per, 2 * HD), BF),
        [VMEM],
        [],
        0,
        2 * part.size * 2,
        "heads",
    )(part)
    return lax.all_to_all(after(blocks, *late), "tensor", split_axis=0, concat_axis=0, tiled=True)


def line_shift(d):
    return [(r, r // 4 * 4 + (r + d) % 4) for r in range(16)]


def plane_shift(d):
    return [(r, (r + 4 * d) % 16) for r in range(16)]


def ring_of(piece, shift):
    return jnp.stack([piece] + [lax.ppermute(piece, "replica", shift(d)) for d in (1, 2, 3)])


def shards(
    patches,
    tile_counts,
    ln_gain,
    enc_qkv,
    enc_out_w,
    proj_w,
    cross_kv_w,
    k_gain,
    plan,
    row_pick,
    q_cross,
    q_self,
    cache_kv,
    new_kv,
    kv_len,
):
    replicas = 16
    group = lax.axis_index("replica")
    pipe = lax.axis_index("pipe")
    tensor = lax.axis_index("tensor")
    images, held, tile_rows, part = patches.shape
    rows = images * held * tile_rows
    order = gather_order(tensor)
    pipe_at = pipe.reshape(1).astype(jnp.int32)

    turned = call(
        turn_kernel, shape_of((part, rows), BF), [VMEM], [], 2 * rows * part * part, 4 * rows * part, "turn"
    )(patches.reshape(rows, part))
    few = out_rows(enc_out_w, group, pipe)
    xs = gather8(turned, after(turned, few))

    turned_w = enc_qkv.transpose(1, 2, 0).reshape(3 * part, ENC_W)
    q, kv = call(
        qkv_kernel,
        (shape_of((part, rows), BF), shape_of((2 * part, rows), BF)),
        [SMEM] + [ANY] * 8 + [VMEM] * 2,
        [pltpu.VMEM((ENC_W, rows), BF), pltpu.SemaphoreType.DMA((8,))],
        2 * rows * ENC_W * 3 * part,
        6 * 1024 * 1024,
        "qkv",
    )(order, *xs, turned_w, ln_gain.reshape(ENC_W, 1))
    kv_other = lax.ppermute(kv, "pipe", [(0, 1), (1, 0)])
    counts_local = lax.dynamic_slice_in_dim(tile_counts, group * images, images)
    mixed = call(
        attend_kernel,
        shape_of((part, rows), BF),
        [SMEM, SMEM, VMEM, VMEM, VMEM],
        [],
        4 * rows * 256 * part,
        2 * 1024 * 1024,
        "encoder_attend",
    )(counts_local, pipe_at, q, kv, kv_other)

    parts = fold_weights(few, proj_w, cross_kv_w, group, pipe, (), ())
    piece = jnp.sum(after(parts, kv).astype(F32), 0).astype(BF)
    line = ring_of(piece, line_shift)
    ms = gather8(mixed)
    plane = ring_of(after(line, mixed), plane_shift)
    spot = jnp.arange(16)
    spot = (group // 4 - spot // 4) % 4 * 4 + (group - spot) % 4
    pieces = jnp.take(after(plane, *ms[5:]).reshape(16, 2, -1, 2 * HD), spot, axis=0)
    pieces = jnp.moveaxis(pieces, 1, 0).reshape(ENC_W, 2 * HD)
    pieces_other = lax.ppermute(pieces, "pipe", [(0, 1), (1, 0)])

    destination = plan[:, 0]
    grouped = destination.reshape(replicas, images)
    earlier = jnp.arange(images)[:, None] < jnp.arange(images)[None, :]
    same_dest = grouped[:, :, None] == grouped[:, None, :]
    ranks = jnp.sum((same_dest & earlier[None]).astype(jnp.int32), 1)
    my_dest = lax.dynamic_index_in_dim(grouped, group, 0, keepdims=False)
    my_rank = lax.dynamic_index_in_dim(ranks, group, 0, keepdims=False)
    spot = my_dest * CAP + my_rank
    picks = jnp.sum(
        jnp.where(
            spot[None, :] == jnp.arange(replicas * CAP)[:, None],
            jnp.arange(images, dtype=jnp.int32)[None, :],
            0,
        ),
        1,
    ).astype(jnp.int32)
    mine = (destination == group).astype(jnp.int32)
    count = jnp.sum(mine)
    before = jnp.cumsum(mine) - mine
    wanted = row_pick % count
    hit = (mine[None, :] == 1) & (before[None, :] == wanted[:, None])
    every = jnp.arange(replicas * images, dtype=jnp.int32)
    slot_of = (every // images) * CAP + ranks.reshape(-1)
    slot_ids = jnp.sum(jnp.where(hit, slot_of[None, :], 0), 1).astype(jnp.int32)
    counts_rows = jnp.sum(jnp.where(hit, tile_counts[None, :], 0), 1).astype(jnp.int32)

    slots = call(
        memory_kernel,
        shape_of((replicas * CAP * held * tile_rows, 2 * HD), BF),
        [SMEM] * 3 + [ANY] * 16 + [VMEM] * 3,
        [
            pltpu.VMEM((ENC_W, rows), BF),
            pltpu.VMEM((ENC_W, rows), BF),
            pltpu.VMEM((rows, 2 * HD), BF),
            pltpu.SemaphoreType.DMA((8,)),
            pltpu.SemaphoreType.DMA((8,)),
        ],
        4 * rows * ENC_W * 2 * HD,
        6 * 1024 * 1024,
        "memory",
    )(order, picks, pipe_at, *xs, *ms, pieces, pieces_other, k_gain.reshape(HD, 1))
    arrived = lax.all_to_all(slots, "replica", split_axis=0, concat_axis=0, tiled=True)
    q_self, q_cross, cache_kv, new_kv, kv_len = (after(v, slots) for v in (q_self, q_cross, cache_kv, new_kv, kv_len))
    rows_here = row_pick.shape[0]
    steps_heads = q_self.shape[0] * q_self.shape[2] // HD

    def heads_of(q):
        return q.reshape(STEPS, rows_here, -1, HD).transpose(1, 0, 2, 3).reshape(rows_here, steps_heads, HD)

    spots = 48
    joined = jnp.concatenate(
        [
            cache_kv.reshape(rows_here, LMAX, 2 * HD),
            jnp.moveaxis(new_kv, 0, 1).reshape(rows_here, STEPS, 2 * HD),
            jnp.zeros((rows_here, spots - LMAX - STEPS, 2 * HD), BF),
        ],
        1,
    )

    def per_head(values):
        return jnp.repeat(values.astype(jnp.int32), steps_heads).reshape(rows_here * steps_heads, 1)

    def scratch(n):
        return [
            pltpu.VMEM((rows_here * steps_heads, n), F32),
            pltpu.VMEM((rows_here * steps_heads, n), BF),
            pltpu.VMEM((rows_here, steps_heads, HD), F32),
        ]

    self_out = call(
        self_kernel,
        shape_of(q_self.shape, BF),
        [VMEM] * 3,
        scratch(spots),
        4 * rows_here * 16 * 128 * 128,
        4 * 1024 * 1024,
        "self_attend",
    )(per_head(kv_len), heads_of(q_self), joined)
    cross_heads, cross_counts = heads_of(q_cross), per_head(counts_rows)
    arrived = after(arrived, self_out, cross_heads, cross_counts, slot_ids)
    arrived_other = lax.ppermute(arrived, "pipe", [(0, 1), (1, 0)])

    cross_out = call(
        cross_kernel,
        shape_of(q_cross.shape, BF),
        [SMEM, SMEM] + [VMEM] * 4,
        scratch(128),
        4 * rows_here * 16 * 128 * 128,
        4 * 1024 * 1024,
        "cross_attend",
    )(slot_ids, pipe_at, cross_counts, cross_heads, arrived, arrived_other)
    return (cross_out, self_out)


def solution(mesh):
    in_specs = (
        P("replica", "pipe", None, "tensor"),
        P(),
        P(),
        P(None, None, "tensor"),
        P("tensor", None),
        P(None, "tensor"),
        P("tensor", None, None),
        P(),
        P(),
        P(("replica", "pipe")),
        P(None, ("replica", "pipe"), "tensor"),
        P(None, ("replica", "pipe"), "tensor"),
        P(("replica", "pipe"), None, None, "tensor"),
        P(None, ("replica", "pipe"), None, "tensor"),
        P(("replica", "pipe")),
    )
    out_specs = (P(None, ("replica", "pipe"), "tensor"), P(None, ("replica", "pipe"), "tensor"))
    return jax.shard_map(shards, mesh=mesh, in_specs=in_specs, out_specs=out_specs, check_vma=False)
```

```python
import functools

import jax
import jax.numpy as jnp
from jax import lax
from jax.experimental import pallas as pl
from jax.experimental.pallas import tpu as pltpu
from jax.sharding import PartitionSpec as P

HEADS = 64
KV_HEADS = 8
HD = 128
ENC_W = 1280
ENC_HEADS = 16
CAP = 2
STEPS = 2
LMAX = 32
TT = 32
LIMIT = 62 * 1024 * 1024
BF = jnp.bfloat16
F32 = jnp.float32

VMEM = pl.BlockSpec(memory_space=pltpu.VMEM)
SMEM = pl.BlockSpec(memory_space=pltpu.SMEM)
ANY = pl.BlockSpec(memory_space=pl.ANY)


def call(kernel, outs, in_specs, scratch, flops, moved, name):
    return pl.pallas_call(
        kernel,
        out_shape=outs,
        in_specs=in_specs,
        out_specs=jax.tree.map(lambda _: VMEM, outs),
        scratch_shapes=scratch,
        compiler_params=pltpu.CompilerParams(vmem_limit_bytes=LIMIT),
        cost_estimate=pl.CostEstimate(flops=flops, bytes_accessed=moved, transcendentals=0),
        name=name,
    )


def shape_of(shape, dtype):
    return jax.ShapeDtypeStruct(shape, dtype)


def dot(a, b, dims):
    return lax.dot_general(a, b, (dims, ((), ())), preferred_element_type=F32)


def turn_kernel(x_ref, out_ref):
    width = x_ref.shape[1]
    row = lax.broadcasted_iota(jnp.int32, (width, width), 0)
    col = lax.broadcasted_iota(jnp.int32, (width, width), 1)
    eye = jnp.where(row == col, 1.0, 0.0).astype(BF)
    out_ref[...] = dot(eye, x_ref[...], ((1,), (1,))).astype(BF)


def qkv_kernel(at_ref, *refs):
    shards = refs[:8]
    w_ref, gain_ref, q_ref, kv_ref, full, sems = refs[8:]
    part, rows = shards[0].shape
    width = part * 8
    fill(at_ref, shards, (full,), (sems,))
    cut = 256
    for j in range(rows // cut):
        lanes = slice(j * cut, (j + 1) * cut)
        base = full[0:1, lanes].astype(F32)
        total, squares = jnp.zeros((1, cut), F32), jnp.zeros((1, cut), F32)
        for i in range(8):
            c = full[i * part : (i + 1) * part, lanes].astype(F32) - base
            total += jnp.sum(c, 0, keepdims=True)
            squares += jnp.sum(c * c, 0, keepdims=True)
        shift = total / width
        mean = base + shift
        scale = lax.rsqrt(jnp.maximum(squares / width - shift * shift, 0.0) + 1e-06)
        for i in range(8):
            at = slice(i * part, (i + 1) * part)
            c = full[at, lanes].astype(F32) - mean
            full[at, lanes] = (c * scale * gain_ref[at, :]).astype(BF)
        out = jnp.dot(w_ref[...], full[:, lanes], preferred_element_type=F32).astype(BF)
        q_ref[:, lanes] = out[:part]
        kv_ref[:, lanes] = out[part:]


def attend_kernel(count_ref, pipe_ref, q_ref, own_ref, other_ref, out_ref):
    part, rows = q_ref.shape
    heads = 2
    hd = part // heads
    pipe, first = pipe_ref[0], pipe_ref[1] * (rows // 64)
    key = lax.broadcasted_iota(jnp.int32, (256, 1), 0)
    from_other = key // 128
    key_image = (key % 128) // 64
    tile = 2 * jnp.where(from_other == 1, 1 - pipe, pipe) + (key % 64) // TT
    lane_image = lax.broadcasted_iota(jnp.int32, (1, 128), 1) // 64
    for j in range(rows // 128):
        lanes = slice(j * 128, (j + 1) * 128)
        count = jnp.where(lane_image == 0, count_ref[first + 2 * j], count_ref[first + 2 * j + 1])
        valid = (key_image == lane_image) & (tile < count)
        for h in range(heads):
            k_at = slice(h * hd, (h + 1) * hd)
            v_at = slice(part + h * hd, part + (h + 1) * hd)
            keys = jnp.concatenate([own_ref[k_at, lanes], other_ref[k_at, lanes]], 1)
            values = jnp.concatenate([own_ref[v_at, lanes], other_ref[v_at, lanes]], 1)
            scores = dot(keys, q_ref[k_at, lanes], ((0,), (0,))) * hd ** (-0.5)
            scores = jnp.where(valid, scores, -1e30)
            weights = jnp.exp(scores - jnp.max(scores, 0, keepdims=True))
            probs = (weights / jnp.sum(weights, 0, keepdims=True)).astype(BF)
            out_ref[k_at, lanes] = jnp.dot(values, probs, preferred_element_type=F32).astype(BF)


def gather_order(t):
    a, b, c = (t + 6) % 8, (t + 2) % 8, (t + 4) % 8
    return [t, t ^ 1, a, b, c, a ^ 1, b ^ 1, c ^ 1]


def fill(at_ref, shards, fulls, sems):
    part = shards[0].shape[0]
    copies = []
    order = gather_order(at_ref[2])
    for i, s in enumerate(shards):
        at = pl.ds(pl.multiple_of(order[i % 8] * part, 16), part)
        copies.append(pltpu.make_async_copy(s, fulls[i // 8].at[at, :], sems[i // 8].at[i % 8]))
    for c in copies:
        c.start()
    for c in copies:
        c.wait()


def memory_kernel(at_ref, pick_ref, *refs):
    xs, ms = refs[:8], refs[8:16]
    w_ref, gain_ref, out_ref, x_ref, m_ref, rows_ref, x_sems, m_sems = refs[16:]
    fill(at_ref, xs + ms, (x_ref, m_ref), (x_sems, m_sems))
    half = w_ref.shape[0] // 4
    mine = pl.ds(pl.multiple_of(at_ref[0] * half, 128), half)
    rest = pl.ds(pl.multiple_of((1 - at_ref[0]) * half, 128), half)
    kv = jnp.zeros((2 * HD, rows_ref.shape[0]), F32)
    for i, rows in enumerate((x_ref[mine, :], m_ref[mine, :], x_ref[rest, :], m_ref[rest, :])):
        kv += dot(w_ref[i * half : (i + 1) * half], rows, ((0,), (0,)))
    keys = kv[:HD]
    keys = keys * lax.rsqrt(jnp.mean(keys * keys, 0, keepdims=True) + 1e-05) * gain_ref[...]
    rows_ref[:, :HD] = jnp.transpose(keys).astype(BF)
    rows_ref[:, HD:] = jnp.transpose(kv[HD:]).astype(BF)
    for i in range(out_ref.shape[0] // 64):
        at = pl.ds(pl.multiple_of(pick_ref[i] * 64, 64), 64)
        out_ref[i * 64 : (i + 1) * 64, :] = rows_ref[at, :]


def finish(score_ref, mixed_ref, valid, out_ref):
    rows = out_ref.shape[1]
    scores = jnp.where(valid, score_ref[...] * HD ** (-0.5), -1e30)
    weights = jnp.exp(scores - jnp.max(scores, 1, keepdims=True))
    return (weights / jnp.sum(weights, 1, keepdims=True)).astype(BF)


def spread(mixed_ref, out_ref):
    group = out_ref.shape[2] // HD
    for s in range(STEPS):
        for h in range(group):
            out_ref[s, :, h * HD : (h + 1) * HD] = mixed_ref[:, s * group + h, :].astype(BF)


def cross_kernel(slot_ref, pipe_ref, count_ref, q_ref, own_ref, other_ref, out_ref, score_ref, prob_ref, mixed_ref):
    rows, per = q_ref.shape[0], q_ref.shape[1]
    pipe = pipe_ref[0]
    for b in range(rows):
        at = pl.ds(pl.multiple_of(slot_ref[b] * 64, 64), 64)
        keys = jnp.concatenate([own_ref[at, :HD], other_ref[at, :HD]], 0)
        score_ref[b * per : (b + 1) * per, :] = dot(q_ref[b], keys, ((1,), (1,)))
    lane = lax.broadcasted_iota(jnp.int32, (1, 128), 1)
    tile = 2 * jnp.where(lane >= 64, 1 - pipe, pipe) + (lane % 64) // TT
    prob_ref[...] = finish(score_ref, mixed_ref, tile < count_ref[...], out_ref)
    for b in range(rows):
        at = pl.ds(pl.multiple_of(slot_ref[b] * 64, 64), 64)
        values = jnp.concatenate([own_ref[at, HD:], other_ref[at, HD:]], 0)
        mixed_ref[b] = jnp.dot(
            prob_ref[b * per : (b + 1) * per, :], values, preferred_element_type=F32
        )
    spread(mixed_ref, out_ref)


def self_kernel(len_ref, q_ref, kv_ref, out_ref, score_ref, prob_ref, mixed_ref):
    rows, per = q_ref.shape[0], q_ref.shape[1]
    for b in range(rows):
        score_ref[b * per : (b + 1) * per, :] = dot(q_ref[b], kv_ref[b, :, :HD], ((1,), (1,)))
    spots = kv_ref.shape[1]
    lane = lax.broadcasted_iota(jnp.int32, (1, spots), 1)
    step = (lax.broadcasted_iota(jnp.int32, (rows * per, 1), 0) % per) // (per // STEPS)
    valid = (lane < len_ref[...]) | ((lane >= LMAX) & (lane <= LMAX + step))
    prob_ref[...] = finish(score_ref, mixed_ref, valid, out_ref)
    for b in range(rows):
        mixed_ref[b] = jnp.dot(
            prob_ref[b * per : (b + 1) * per, :], kv_ref[b, :, HD:], preferred_element_type=F32
        )
    spread(mixed_ref, out_ref)


ZX = [(t, t ^ 1) for t in range(8)]


def y_perm(d):
    return [(t, (t + 2 * d) % 8) for t in range(8)]


def gather8(s, near, hold):
    p1, p2, p3 = y_perm(1), y_perm(2), y_perm(3)
    z = lax.ppermute(s, "tensor", ZX)
    a, b, c = (lax.ppermute(near, "tensor", p) for p in (p1, p3, p2))
    z = after(z, *hold(a, b, c))
    za, zb, zc = (lax.ppermute(z, "tensor", p) for p in (p1, p3, p2))
    return (s, z, a, b, c, za, zb, zc)


def after(value, *others):
    return lax.optimization_barrier((value,) + others)[0]


def swap(values, axis, bit, size):
    return lax.ppermute(values, axis, [(i, i ^ bit) for i in range(size)])


def choose(flag, a, b):
    return jnp.where(flag, a, b)


def out_rows(enc_out_w, replica, pipe):
    per = ENC_W // 32
    pairs = []
    for r in range(16):
        for p in range(2):
            for t in range(8):
                part = p * 4 + r // 4
                near = t % 2 == part % 2
                source = t // 2 * 4 + (r % 4 if near else 3 - r % 4)
                core = 0 if near else 1
                pairs.append(((source * 2 + core) * 8 + part, (r * 2 + p) * 8 + t))
    block = jnp.where(pipe == 0, replica % 4, 3 - replica % 4)
    mine = lax.dynamic_slice_in_dim(enc_out_w, block * per, per)
    return lax.ppermute(mine, ("replica", "pipe", "tensor"), pairs)


def heads_kernel(part_ref, out_ref):
    for h in range(KV_HEADS):
        out_ref[h, :, :HD] = part_ref[0, :, h * HD : (h + 1) * HD]
        out_ref[h, :, HD:] = part_ref[1, :, h * HD : (h + 1) * HD]


def fold_weights(few, proj_w, cross_kv_w, replica, pipe):
    per = ENC_W // 32
    folded = jnp.dot(few, proj_w, preferred_element_type=F32).astype(BF)
    left = lax.dynamic_slice_in_dim(proj_w, (pipe * 16 + replica) * per, per)
    left = jnp.concatenate([left, folded], 0)
    part = jnp.einsum("rk,kcn->crn", left, cross_kv_w, preferred_element_type=F32).astype(BF)
    return call(
        heads_kernel,
        shape_of((KV_HEADS, 2 * per, 2 * HD), BF),
        [VMEM],
        [],
        0,
        2 * part.size * 2,
        "heads",
    )(part)


def line_shift(d):
    return [(r, r // 4 * 4 + (r + d) % 4) for r in range(16)]


def plane_shift(d):
    return [(r, (r + 4 * d) % 16) for r in range(16)]


def ring_of(piece, shift):
    return jnp.stack([piece] + [lax.ppermute(piece, "replica", shift(d)) for d in (1, 2, 3)])


def shards(
    patches,
    tile_counts,
    ln_gain,
    enc_qkv,
    enc_out_w,
    proj_w,
    cross_kv_w,
    k_gain,
    plan,
    row_pick,
    q_cross,
    q_self,
    cache_kv,
    new_kv,
    kv_len,
):
    replicas = 16
    group = lax.axis_index("replica")
    pipe = lax.axis_index("pipe")
    tensor = lax.axis_index("tensor")
    images, held, tile_rows, part = patches.shape
    rows = images * held * tile_rows
    pipe_at = jnp.stack([pipe, group, tensor]).astype(jnp.int32)

    turned = call(
        turn_kernel, shape_of((part, rows), BF), [VMEM], [], 2 * rows * part * part, 4 * rows * part, "turn"
    )(patches.reshape(rows, part))
    few = out_rows(enc_out_w, group, pipe)
    blocks = fold_weights(few, proj_w, cross_kv_w, group, pipe)
    norm_gain = ln_gain.reshape(ENC_W, 1)
    xs = gather8(turned, after(turned, few, norm_gain), lambda *_: (blocks,))

    turned_w = enc_qkv.transpose(1, 2, 0).reshape(3 * part, ENC_W)
    q, kv = call(
        qkv_kernel,
        (shape_of((part, rows), BF), shape_of((2 * part, rows), BF)),
        [SMEM] + [ANY] * 8 + [VMEM] * 2,
        [pltpu.VMEM((ENC_W, rows), BF), pltpu.SemaphoreType.DMA((8,))],
        2 * rows * ENC_W * 3 * part,
        6 * 1024 * 1024,
        "qkv",
    )(pipe_at, *xs, turned_w, norm_gain)
    kv_other = lax.ppermute(kv, "pipe", [(0, 1), (1, 0)])
    mixed = call(
        attend_kernel,
        shape_of((part, rows), BF),
        [SMEM, SMEM, VMEM, VMEM, VMEM],
        [],
        4 * rows * 256 * part,
        2 * 1024 * 1024,
        "encoder_attend",
    )(tile_counts, pipe_at, q, kv, kv_other)

    parts = lax.all_to_all(blocks, "tensor", split_axis=0, concat_axis=0, tiled=True)
    piece = jnp.sum(after(parts, kv).astype(F32), 0).astype(BF)
    line = ring_of(piece, line_shift)
    ms = gather8(mixed, mixed, lambda *abc: abc)
    line_other = lax.ppermute(line, "pipe", [(0, 1), (1, 0)])
    plane = ring_of(after(jnp.stack([line, line_other]), mixed), plane_shift)
    spot = jnp.arange(16)
    spot = (group // 4 - spot // 4) % 4 * 4 + (group - spot) % 4
    plane = jnp.moveaxis(plane, 1, 0).reshape(2, 16, 2, -1, 2 * HD)
    pieces = jnp.moveaxis(jnp.take(plane, spot, axis=1), 2, 1).reshape(2 * ENC_W, 2 * HD)

    destination = after(plan, ms[1])[:, 0]
    grouped = destination.reshape(replicas, images)
    earlier = jnp.arange(images)[:, None] < jnp.arange(images)[None, :]
    same_dest = grouped[:, :, None] == grouped[:, None, :]
    ranks = jnp.sum((same_dest & earlier[None]).astype(jnp.int32), 1)
    my_dest = lax.dynamic_index_in_dim(grouped, group, 0, keepdims=False)
    my_rank = lax.dynamic_index_in_dim(ranks, group, 0, keepdims=False)
    spot = my_dest * CAP + my_rank
    picks = jnp.sum(
        jnp.where(
            spot[None, :] == jnp.arange(replicas * CAP)[:, None],
            jnp.arange(images, dtype=jnp.int32)[None, :],
            0,
        ),
        1,
    ).astype(jnp.int32)
    mine = (destination == group).astype(jnp.int32)
    count = jnp.sum(mine)
    before = jnp.cumsum(mine) - mine
    wanted = row_pick % count
    hit = (mine[None, :] == 1) & (before[None, :] == wanted[:, None])
    every = jnp.arange(replicas * images, dtype=jnp.int32)
    slot_of = (every // images) * CAP + ranks.reshape(-1)
    slot_ids = jnp.sum(jnp.where(hit, slot_of[None, :], 0), 1).astype(jnp.int32)
    counts_rows = jnp.sum(jnp.where(hit, tile_counts[None, :], 0), 1).astype(jnp.int32)
    gain = k_gain.reshape(HD, 1)
    slots = call(
        memory_kernel,
        shape_of((replicas * CAP * held * tile_rows, 2 * HD), BF),
        [SMEM] * 2 + [ANY] * 16 + [VMEM] * 2,
        [
            pltpu.VMEM((ENC_W, rows), BF),
            pltpu.VMEM((ENC_W, rows), BF),
            pltpu.VMEM((rows, 2 * HD), BF),
            pltpu.SemaphoreType.DMA((8,)),
            pltpu.SemaphoreType.DMA((8,)),
        ],
        4 * rows * ENC_W * 2 * HD,
        6 * 1024 * 1024,
        "memory",
    )(pipe_at, picks, *xs, *ms, pieces, gain)
    arrived = lax.all_to_all(slots, "replica", split_axis=0, concat_axis=0, tiled=True)
    q_self, q_cross, cache_kv, new_kv, kv_len = (after(v, slots) for v in (q_self, q_cross, cache_kv, new_kv, kv_len))
    rows_here = row_pick.shape[0]
    steps_heads = q_self.shape[0] * q_self.shape[2] // HD

    def heads_of(q):
        return q.reshape(STEPS, rows_here, -1, HD).transpose(1, 0, 2, 3).reshape(rows_here, steps_heads, HD)

    spots = 48
    joined = jnp.concatenate(
        [
            cache_kv.reshape(rows_here, LMAX, 2 * HD),
            jnp.moveaxis(new_kv, 0, 1).reshape(rows_here, STEPS, 2 * HD),
            jnp.zeros((rows_here, spots - LMAX - STEPS, 2 * HD), BF),
        ],
        1,
    )

    def per_head(values):
        return jnp.repeat(values.astype(jnp.int32), steps_heads).reshape(rows_here * steps_heads, 1)

    def scratch(n):
        return [
            pltpu.VMEM((rows_here * steps_heads, n), F32),
            pltpu.VMEM((rows_here * steps_heads, n), BF),
            pltpu.VMEM((rows_here, steps_heads, HD), F32),
        ]

    self_out = call(
        self_kernel,
        shape_of(q_self.shape, BF),
        [VMEM] * 3,
        scratch(spots),
        4 * rows_here * 16 * 128 * 128,
        4 * 1024 * 1024,
        "self_attend",
    )(per_head(kv_len), heads_of(q_self), joined)
    cross_heads, cross_counts = heads_of(q_cross), per_head(counts_rows)
    arrived = after(arrived, self_out, cross_heads, cross_counts, slot_ids)
    arrived_other = lax.ppermute(arrived, "pipe", [(0, 1), (1, 0)])

    cross_out = call(
        cross_kernel,
        shape_of(q_cross.shape, BF),
        [SMEM, SMEM] + [VMEM] * 4,
        scratch(128),
        4 * rows_here * 16 * 128 * 128,
        4 * 1024 * 1024,
        "cross_attend",
    )(slot_ids, pipe_at, cross_counts, cross_heads, arrived, arrived_other)
    return (cross_out, self_out)


def solution(mesh):
    in_specs = (
        P("replica", "pipe", None, "tensor"),
        P(),
        P(),
        P(None, None, "tensor"),
        P("tensor", None),
        P(None, "tensor"),
        P("tensor", None, None),
        P(),
        P(),
        P(("replica", "pipe")),
        P(None, ("replica", "pipe"), "tensor"),
        P(None, ("replica", "pipe"), "tensor"),
        P(("replica", "pipe"), None, None, "tensor"),
        P(None, ("replica", "pipe"), None, "tensor"),
        P(("replica", "pipe")),
    )
    out_specs = (P(None, ("replica", "pipe"), "tensor"), P(None, ("replica", "pipe"), "tensor"))
    return jax.shard_map(shards, mesh=mesh, in_specs=in_specs, out_specs=out_specs, check_vma=False)
```

```python
import functools

import jax
import jax.numpy as jnp
from jax import lax
from jax.experimental import pallas as pl
from jax.experimental.pallas import tpu as pltpu
from jax.sharding import PartitionSpec as P

HEADS = 64
KV_HEADS = 8
HD = 128
ENC_W = 1280
ENC_HEADS = 16
CAP = 2
STEPS = 2
LMAX = 32
TT = 32
LIMIT = 62 * 1024 * 1024
BF = jnp.bfloat16
F32 = jnp.float32

VMEM = pl.BlockSpec(memory_space=pltpu.VMEM)
SMEM = pl.BlockSpec(memory_space=pltpu.SMEM)
ANY = pl.BlockSpec(memory_space=pl.ANY)


def call(kernel, outs, in_specs, scratch, flops, moved, name):
    return pl.pallas_call(
        kernel,
        out_shape=outs,
        in_specs=in_specs,
        out_specs=jax.tree.map(lambda _: VMEM, outs),
        scratch_shapes=scratch,
        compiler_params=pltpu.CompilerParams(vmem_limit_bytes=LIMIT),
        cost_estimate=pl.CostEstimate(flops=flops, bytes_accessed=moved, transcendentals=0),
        name=name,
    )


def shape_of(shape, dtype):
    return jax.ShapeDtypeStruct(shape, dtype)


def dot(a, b, dims):
    return lax.dot_general(a, b, (dims, ((), ())), preferred_element_type=F32)


def turn_kernel(x_ref, out_ref):
    width = x_ref.shape[1]
    row = lax.broadcasted_iota(jnp.int32, (width, width), 0)
    col = lax.broadcasted_iota(jnp.int32, (width, width), 1)
    eye = jnp.where(row == col, 1.0, 0.0).astype(BF)
    out_ref[...] = dot(eye, x_ref[...], ((1,), (1,))).astype(BF)


def qkv_kernel(at_ref, *refs):
    shards = refs[:8]
    w_ref, gain_ref, q_ref, kv_ref, full, sems = refs[8:]
    part, rows = shards[0].shape
    width = part * 8
    fill(at_ref, shards, (full,), (sems,))
    cut = 256
    for j in range(rows // cut):
        lanes = slice(j * cut, (j + 1) * cut)
        base = full[0:1, lanes].astype(F32)
        total, squares = jnp.zeros((1, cut), F32), jnp.zeros((1, cut), F32)
        for i in range(8):
            c = full[i * part : (i + 1) * part, lanes].astype(F32) - base
            total += jnp.sum(c, 0, keepdims=True)
            squares += jnp.sum(c * c, 0, keepdims=True)
        shift = total / width
        mean = base + shift
        scale = lax.rsqrt(jnp.maximum(squares / width - shift * shift, 0.0) + 1e-06)
        for i in range(8):
            at = slice(i * part, (i + 1) * part)
            c = full[at, lanes].astype(F32) - mean
            full[at, lanes] = (c * scale * gain_ref[at, :]).astype(BF)
        out = jnp.dot(w_ref[...], full[:, lanes], preferred_element_type=F32).astype(BF)
        q_ref[:, lanes] = out[:part]
        kv_ref[:, lanes] = out[part:]


def attend_kernel(count_ref, pipe_ref, q_ref, own_ref, other_ref, out_ref):
    part, rows = q_ref.shape
    heads = 2
    hd = part // heads
    pipe, first = pipe_ref[0], pipe_ref[1] * (rows // 64)
    key = lax.broadcasted_iota(jnp.int32, (256, 1), 0)
    from_other = key // 128
    key_image = (key % 128) // 64
    tile = 2 * jnp.where(from_other == 1, 1 - pipe, pipe) + (key % 64) // TT
    lane_image = lax.broadcasted_iota(jnp.int32, (1, 128), 1) // 64
    for j in range(rows // 128):
        lanes = slice(j * 128, (j + 1) * 128)
        count = jnp.where(lane_image == 0, count_ref[first + 2 * j], count_ref[first + 2 * j + 1])
        valid = (key_image == lane_image) & (tile < count)
        for h in range(heads):
            k_at = slice(h * hd, (h + 1) * hd)
            v_at = slice(part + h * hd, part + (h + 1) * hd)
            keys = jnp.concatenate([own_ref[k_at, lanes], other_ref[k_at, lanes]], 1)
            values = jnp.concatenate([own_ref[v_at, lanes], other_ref[v_at, lanes]], 1)
            scores = dot(keys, q_ref[k_at, lanes], ((0,), (0,))) * hd ** (-0.5)
            scores = jnp.where(valid, scores, -1e30)
            weights = jnp.exp(scores - jnp.max(scores, 0, keepdims=True))
            probs = (weights / jnp.sum(weights, 0, keepdims=True)).astype(BF)
            out_ref[k_at, lanes] = jnp.dot(values, probs, preferred_element_type=F32).astype(BF)


def gather_order(t):
    a, b, c = (t + 6) % 8, (t + 2) % 8, (t + 4) % 8
    return [t, t ^ 1, a, b, c, a ^ 1, b ^ 1, c ^ 1]


def fill(at_ref, shards, fulls, sems):
    part = shards[0].shape[0]
    copies = []
    order = gather_order(at_ref[2])
    for i, s in enumerate(shards):
        at = pl.ds(pl.multiple_of(order[i % 8] * part, 16), part)
        copies.append(pltpu.make_async_copy(s, fulls[i // 8].at[at, :], sems[i // 8].at[i % 8]))
    for c in copies:
        c.start()
    for c in copies:
        c.wait()


def memory_kernel(at_ref, pick_ref, *refs):
    xs, ms = refs[:8], refs[8:16]
    w_ref, gain_ref, out_ref, x_ref, m_ref, rows_ref, x_sems, m_sems = refs[16:]
    fill(at_ref, xs + ms, (x_ref, m_ref), (x_sems, m_sems))
    half = w_ref.shape[0] // 4
    mine = pl.ds(pl.multiple_of(at_ref[0] * half, 128), half)
    rest = pl.ds(pl.multiple_of((1 - at_ref[0]) * half, 128), half)
    kv = jnp.zeros((2 * HD, rows_ref.shape[0]), F32)
    for i, rows in enumerate((x_ref[mine, :], m_ref[mine, :], x_ref[rest, :], m_ref[rest, :])):
        kv += dot(w_ref[i * half : (i + 1) * half], rows, ((0,), (0,)))
    keys = kv[:HD]
    keys = keys * lax.rsqrt(jnp.mean(keys * keys, 0, keepdims=True) + 1e-05) * gain_ref[...]
    rows_ref[:, :HD] = jnp.transpose(keys).astype(BF)
    rows_ref[:, HD:] = jnp.transpose(kv[HD:]).astype(BF)
    for i in range(out_ref.shape[0] // 64):
        at = pl.ds(pl.multiple_of(pick_ref[i] * 64, 64), 64)
        out_ref[i * 64 : (i + 1) * 64, :] = rows_ref[at, :]


def finish(score_ref, mixed_ref, valid, out_ref):
    rows = out_ref.shape[1]
    scores = jnp.where(valid, score_ref[...] * HD ** (-0.5), -1e30)
    weights = jnp.exp(scores - jnp.max(scores, 1, keepdims=True))
    return (weights / jnp.sum(weights, 1, keepdims=True)).astype(BF)


def spread(mixed_ref, out_ref):
    group = out_ref.shape[2] // HD
    for s in range(STEPS):
        for h in range(group):
            out_ref[s, :, h * HD : (h + 1) * HD] = mixed_ref[:, s * group + h, :].astype(BF)


def cross_kernel(slot_ref, pipe_ref, count_ref, q_ref, own_ref, other_ref, out_ref, score_ref, prob_ref, mixed_ref):
    rows, per = q_ref.shape[0], q_ref.shape[1]
    pipe = pipe_ref[0]
    for b in range(rows):
        at = pl.ds(pl.multiple_of(slot_ref[b] * 64, 64), 64)
        keys = jnp.concatenate([own_ref[at, :HD], other_ref[at, :HD]], 0)
        score_ref[b * per : (b + 1) * per, :] = dot(q_ref[b], keys, ((1,), (1,)))
    lane = lax.broadcasted_iota(jnp.int32, (1, 128), 1)
    tile = 2 * jnp.where(lane >= 64, 1 - pipe, pipe) + (lane % 64) // TT
    prob_ref[...] = finish(score_ref, mixed_ref, tile < count_ref[...], out_ref)
    for b in range(rows):
        at = pl.ds(pl.multiple_of(slot_ref[b] * 64, 64), 64)
        values = jnp.concatenate([own_ref[at, HD:], other_ref[at, HD:]], 0)
        mixed_ref[b] = jnp.dot(
            prob_ref[b * per : (b + 1) * per, :], values, preferred_element_type=F32
        )
    spread(mixed_ref, out_ref)


def self_kernel(len_ref, q_ref, kv_ref, out_ref, score_ref, prob_ref, mixed_ref):
    rows, per = q_ref.shape[0], q_ref.shape[1]
    for b in range(rows):
        score_ref[b * per : (b + 1) * per, :] = dot(q_ref[b], kv_ref[b, :, :HD], ((1,), (1,)))
    spots = kv_ref.shape[1]
    lane = lax.broadcasted_iota(jnp.int32, (1, spots), 1)
    step = (lax.broadcasted_iota(jnp.int32, (rows * per, 1), 0) % per) // (per // STEPS)
    valid = (lane < len_ref[...]) | ((lane >= LMAX) & (lane <= LMAX + step))
    prob_ref[...] = finish(score_ref, mixed_ref, valid, out_ref)
    for b in range(rows):
        mixed_ref[b] = jnp.dot(
            prob_ref[b * per : (b + 1) * per, :], kv_ref[b, :, HD:], preferred_element_type=F32
        )
    spread(mixed_ref, out_ref)


ZX = [(t, t ^ 1) for t in range(8)]


def y_perm(d):
    return [(t, (t + 2 * d) % 8) for t in range(8)]


def gather8(s, near, hold):
    p1, p2, p3 = y_perm(1), y_perm(2), y_perm(3)
    z = lax.ppermute(s, "tensor", ZX)
    a, b, c = (lax.ppermute(near, "tensor", p) for p in (p1, p3, p2))
    z = after(z, *hold(a, b, c))
    za, zb, zc = (lax.ppermute(z, "tensor", p) for p in (p1, p3, p2))
    return (s, z, a, b, c, za, zb, zc)


def after(value, *others):
    return lax.optimization_barrier((value,) + others)[0]


def swap(values, axis, bit, size):
    return lax.ppermute(values, axis, [(i, i ^ bit) for i in range(size)])


def choose(flag, a, b):
    return jnp.where(flag, a, b)


def out_rows(enc_out_w, replica, pipe):
    per = ENC_W // 32
    pairs = []
    for r in range(16):
        for p in range(2):
            for t in range(8):
                part = p * 4 + r // 4
                near = t % 2 == part % 2
                source = t // 2 * 4 + (r % 4 if near else 3 - r % 4)
                core = 0 if near else 1
                pairs.append(((source * 2 + core) * 8 + part, (r * 2 + p) * 8 + t))
    block = jnp.where(pipe == 0, replica % 4, 3 - replica % 4)
    mine = lax.dynamic_slice_in_dim(enc_out_w, block * per, per)
    return lax.ppermute(mine, ("replica", "pipe", "tensor"), pairs)


def heads_kernel(part_ref, out_ref):
    for h in range(KV_HEADS):
        out_ref[h, :, :HD] = part_ref[0, :, h * HD : (h + 1) * HD]
        out_ref[h, :, HD:] = part_ref[1, :, h * HD : (h + 1) * HD]


def fold_weights(few, proj_w, cross_kv_w, replica, pipe):
    per = ENC_W // 32
    folded = jnp.dot(few, proj_w, preferred_element_type=F32).astype(BF)
    left = lax.dynamic_slice_in_dim(proj_w, (pipe * 16 + replica) * per, per)
    left = jnp.concatenate([left, folded], 0)
    part = jnp.einsum("rk,kcn->crn", left, cross_kv_w, preferred_element_type=F32).astype(BF)
    return call(
        heads_kernel,
        shape_of((KV_HEADS, 2 * per, 2 * HD), BF),
        [VMEM],
        [],
        0,
        2 * part.size * 2,
        "heads",
    )(part)


def line_shift(d):
    return [(r, r // 4 * 4 + (r + d) % 4) for r in range(16)]


def plane_shift(d):
    return [(r, (r + 4 * d) % 16) for r in range(16)]


def ring_of(piece, shift):
    return jnp.stack([piece] + [lax.ppermute(piece, "replica", shift(d)) for d in (1, 2, 3)])


def shards(
    patches,
    tile_counts,
    ln_gain,
    enc_qkv,
    enc_out_w,
    proj_w,
    cross_kv_w,
    k_gain,
    plan,
    row_pick,
    q_cross,
    q_self,
    cache_kv,
    new_kv,
    kv_len,
):
    replicas = 16
    group = lax.axis_index("replica")
    pipe = lax.axis_index("pipe")
    tensor = lax.axis_index("tensor")
    images, held, tile_rows, part = patches.shape
    rows = images * held * tile_rows
    pipe_at = jnp.stack([pipe, group, tensor]).astype(jnp.int32)

    turned = call(
        turn_kernel, shape_of((part, rows), BF), [VMEM], [], 2 * rows * part * part, 4 * rows * part, "turn"
    )(patches.reshape(rows, part))
    few = out_rows(enc_out_w, group, pipe)
    blocks = fold_weights(few, proj_w, cross_kv_w, group, pipe)
    norm_gain = ln_gain.reshape(ENC_W, 1)
    xs = gather8(turned, after(turned, few, norm_gain), lambda *_: (blocks,))

    turned_w = enc_qkv.transpose(1, 2, 0).reshape(3 * part, ENC_W)
    q, kv = call(
        qkv_kernel,
        (shape_of((part, rows), BF), shape_of((2 * part, rows), BF)),
        [SMEM] + [ANY] * 8 + [VMEM] * 2,
        [pltpu.VMEM((ENC_W, rows), BF), pltpu.SemaphoreType.DMA((8,))],
        2 * rows * ENC_W * 3 * part,
        6 * 1024 * 1024,
        "qkv",
    )(pipe_at, *xs, turned_w, norm_gain)
    kv_other = lax.ppermute(kv, "pipe", [(0, 1), (1, 0)])
    mixed = call(
        attend_kernel,
        shape_of((part, rows), BF),
        [SMEM, SMEM, VMEM, VMEM, VMEM],
        [],
        4 * rows * 256 * part,
        2 * 1024 * 1024,
        "encoder_attend",
    )(tile_counts, pipe_at, q, kv, kv_other)

    parts = lax.all_to_all(blocks, "tensor", split_axis=0, concat_axis=0, tiled=True)
    piece = jnp.sum(after(parts, kv).astype(F32), 0).astype(BF)
    line = ring_of(piece, line_shift)
    ms = gather8(mixed, mixed, lambda *abc: abc)
    line = after(line, mixed)
    line_other = lax.ppermute(line, "pipe", [(0, 1), (1, 0)])
    plane = ring_of(after(jnp.stack([line, line_other]), mixed), plane_shift)
    spot = jnp.arange(16)
    spot = (group // 4 - spot // 4) % 4 * 4 + (group - spot) % 4
    plane = jnp.moveaxis(plane, 1, 0).reshape(2, 16, 2, -1, 2 * HD)
    pieces = jnp.moveaxis(jnp.take(plane, spot, axis=1), 2, 1).reshape(2 * ENC_W, 2 * HD)

    destination = after(plan, ms[1])[:, 0]
    grouped = destination.reshape(replicas, images)
    earlier = jnp.arange(images)[:, None] < jnp.arange(images)[None, :]
    same_dest = grouped[:, :, None] == grouped[:, None, :]
    ranks = jnp.sum((same_dest & earlier[None]).astype(jnp.int32), 1)
    my_dest = lax.dynamic_index_in_dim(grouped, group, 0, keepdims=False)
    my_rank = lax.dynamic_index_in_dim(ranks, group, 0, keepdims=False)
    spot = my_dest * CAP + my_rank
    picks = jnp.sum(
        jnp.where(
            spot[None, :] == jnp.arange(replicas * CAP)[:, None],
            jnp.arange(images, dtype=jnp.int32)[None, :],
            0,
        ),
        1,
    ).astype(jnp.int32)
    mine = (destination == group).astype(jnp.int32)
    count = jnp.sum(mine)
    before = jnp.cumsum(mine) - mine
    wanted = row_pick % count
    hit = (mine[None, :] == 1) & (before[None, :] == wanted[:, None])
    every = jnp.arange(replicas * images, dtype=jnp.int32)
    slot_of = (every // images) * CAP + ranks.reshape(-1)
    slot_ids = jnp.sum(jnp.where(hit, slot_of[None, :], 0), 1).astype(jnp.int32)
    counts_rows = jnp.sum(jnp.where(hit, tile_counts[None, :], 0), 1).astype(jnp.int32)
    gain = k_gain.reshape(HD, 1)
    slots = call(
        memory_kernel,
        shape_of((replicas * CAP * held * tile_rows, 2 * HD), BF),
        [SMEM] * 2 + [ANY] * 16 + [VMEM] * 2,
        [
            pltpu.VMEM((ENC_W, rows), BF),
            pltpu.VMEM((ENC_W, rows), BF),
            pltpu.VMEM((rows, 2 * HD), BF),
            pltpu.SemaphoreType.DMA((8,)),
            pltpu.SemaphoreType.DMA((8,)),
        ],
        4 * rows * ENC_W * 2 * HD,
        6 * 1024 * 1024,
        "memory",
    )(pipe_at, picks, *xs, *ms, pieces, gain)
    arrived = lax.all_to_all(slots, "replica", split_axis=0, concat_axis=0, tiled=True)
    q_self, q_cross, cache_kv, new_kv, kv_len = (after(v, slots) for v in (q_self, q_cross, cache_kv, new_kv, kv_len))
    rows_here = row_pick.shape[0]
    steps_heads = q_self.shape[0] * q_self.shape[2] // HD

    def heads_of(q):
        return q.reshape(STEPS, rows_here, -1, HD).transpose(1, 0, 2, 3).reshape(rows_here, steps_heads, HD)

    spots = 48
    joined = jnp.concatenate(
        [
            cache_kv.reshape(rows_here, LMAX, 2 * HD),
            jnp.moveaxis(new_kv, 0, 1).reshape(rows_here, STEPS, 2 * HD),
            jnp.zeros((rows_here, spots - LMAX - STEPS, 2 * HD), BF),
        ],
        1,
    )

    def per_head(values):
        return jnp.repeat(values.astype(jnp.int32), steps_heads).reshape(rows_here * steps_heads, 1)

    def scratch(n):
        return [
            pltpu.VMEM((rows_here * steps_heads, n), F32),
            pltpu.VMEM((rows_here * steps_heads, n), BF),
            pltpu.VMEM((rows_here, steps_heads, HD), F32),
        ]

    self_out = call(
        self_kernel,
        shape_of(q_self.shape, BF),
        [VMEM] * 3,
        scratch(spots),
        4 * rows_here * 16 * 128 * 128,
        4 * 1024 * 1024,
        "self_attend",
    )(per_head(kv_len), heads_of(q_self), joined)
    cross_heads, cross_counts = heads_of(q_cross), per_head(counts_rows)
    arrived = after(arrived, self_out, cross_heads, cross_counts, slot_ids)
    arrived_other = lax.ppermute(arrived, "pipe", [(0, 1), (1, 0)])

    cross_out = call(
        cross_kernel,
        shape_of(q_cross.shape, BF),
        [SMEM, SMEM] + [VMEM] * 4,
        scratch(128),
        4 * rows_here * 16 * 128 * 128,
        4 * 1024 * 1024,
        "cross_attend",
    )(slot_ids, pipe_at, cross_counts, cross_heads, arrived, arrived_other)
    return (cross_out, self_out)


def solution(mesh):
    in_specs = (
        P("replica", "pipe", None, "tensor"),
        P(),
        P(),
        P(None, None, "tensor"),
        P("tensor", None),
        P(None, "tensor"),
        P("tensor", None, None),
        P(),
        P(),
        P(("replica", "pipe")),
        P(None, ("replica", "pipe"), "tensor"),
        P(None, ("replica", "pipe"), "tensor"),
        P(("replica", "pipe"), None, None, "tensor"),
        P(None, ("replica", "pipe"), None, "tensor"),
        P(("replica", "pipe")),
    )
    out_specs = (P(None, ("replica", "pipe"), "tensor"), P(None, ("replica", "pipe"), "tensor"))
    return jax.shard_map(shards, mesh=mesh, in_specs=in_specs, out_specs=out_specs, check_vma=False)
```

```python
import functools

import jax
import jax.numpy as jnp
from jax import lax
from jax.experimental import pallas as pl
from jax.experimental.pallas import tpu as pltpu
from jax.sharding import PartitionSpec as P

HEADS = 64
KV_HEADS = 8
HD = 128
ENC_W = 1280
ENC_HEADS = 16
CAP = 2
STEPS = 2
LMAX = 32
TT = 32
LIMIT = 62 * 1024 * 1024
BF = jnp.bfloat16
F32 = jnp.float32

VMEM = pl.BlockSpec(memory_space=pltpu.VMEM)
SMEM = pl.BlockSpec(memory_space=pltpu.SMEM)
ANY = pl.BlockSpec(memory_space=pl.ANY)


def call(kernel, outs, in_specs, scratch, flops, moved, name):
    return pl.pallas_call(
        kernel,
        out_shape=outs,
        in_specs=in_specs,
        out_specs=jax.tree.map(lambda _: VMEM, outs),
        scratch_shapes=scratch,
        compiler_params=pltpu.CompilerParams(vmem_limit_bytes=LIMIT),
        cost_estimate=pl.CostEstimate(flops=flops, bytes_accessed=moved, transcendentals=0),
        name=name,
    )


def shape_of(shape, dtype):
    return jax.ShapeDtypeStruct(shape, dtype)


def dot(a, b, dims):
    return lax.dot_general(a, b, (dims, ((), ())), preferred_element_type=F32)


def turn_kernel(x_ref, out_ref):
    width = x_ref.shape[1]
    row = lax.broadcasted_iota(jnp.int32, (width, width), 0)
    col = lax.broadcasted_iota(jnp.int32, (width, width), 1)
    eye = jnp.where(row == col, 1.0, 0.0).astype(BF)
    out_ref[...] = dot(eye, x_ref[...], ((1,), (1,))).astype(BF)


def qkv_kernel(at_ref, *refs):
    shards = refs[:8]
    w_in, gain_in, q_ref, kv_ref, full, w_ref, gain_ref, sems, more = refs[8:]
    part, rows = shards[0].shape
    width = part * 8
    extra = [
        pltpu.make_async_copy(gain_in, gain_ref, more.at[0]),
        pltpu.make_async_copy(w_in, w_ref, more.at[1]),
    ]
    for c in extra:
        c.start()
    fill(at_ref, shards, (full,), (sems,))
    for c in extra:
        c.wait()
    cut = 256
    for j in range(rows // cut):
        lanes = slice(j * cut, (j + 1) * cut)
        base = full[0:1, lanes].astype(F32)
        total, squares = jnp.zeros((1, cut), F32), jnp.zeros((1, cut), F32)
        for i in range(8):
            c = full[i * part : (i + 1) * part, lanes].astype(F32) - base
            total += jnp.sum(c, 0, keepdims=True)
            squares += jnp.sum(c * c, 0, keepdims=True)
        shift = total / width
        mean = base + shift
        scale = lax.rsqrt(jnp.maximum(squares / width - shift * shift, 0.0) + 1e-06)
        for i in range(8):
            at = slice(i * part, (i + 1) * part)
            c = full[at, lanes].astype(F32) - mean
            full[at, lanes] = (c * scale * gain_ref[at, :]).astype(BF)
        out = jnp.dot(w_ref[...], full[:, lanes], preferred_element_type=F32).astype(BF)
        q_ref[:, lanes] = out[:part]
        kv_ref[:, lanes] = out[part:]


def attend_kernel(count_ref, pipe_ref, q_ref, own_ref, other_ref, out_ref):
    part, rows = q_ref.shape
    heads = 2
    hd = part // heads
    pipe, first = pipe_ref[0], pipe_ref[1] * (rows // 64)
    key = lax.broadcasted_iota(jnp.int32, (256, 1), 0)
    from_other = key // 128
    key_image = (key % 128) // 64
    tile = 2 * jnp.where(from_other == 1, 1 - pipe, pipe) + (key % 64) // TT
    lane_image = lax.broadcasted_iota(jnp.int32, (1, 128), 1) // 64
    for j in range(rows // 128):
        lanes = slice(j * 128, (j + 1) * 128)
        count = jnp.where(lane_image == 0, count_ref[first + 2 * j], count_ref[first + 2 * j + 1])
        valid = (key_image == lane_image) & (tile < count)
        for h in range(heads):
            k_at = slice(h * hd, (h + 1) * hd)
            v_at = slice(part + h * hd, part + (h + 1) * hd)
            keys = jnp.concatenate([own_ref[k_at, lanes], other_ref[k_at, lanes]], 1)
            values = jnp.concatenate([own_ref[v_at, lanes], other_ref[v_at, lanes]], 1)
            scores = dot(keys, q_ref[k_at, lanes], ((0,), (0,))) * hd ** (-0.5)
            scores = jnp.where(valid, scores, -1e30)
            weights = jnp.exp(scores - jnp.max(scores, 0, keepdims=True))
            probs = (weights / jnp.sum(weights, 0, keepdims=True)).astype(BF)
            out_ref[k_at, lanes] = jnp.dot(values, probs, preferred_element_type=F32).astype(BF)


def gather_order(t):
    a, b, c = (t + 6) % 8, (t + 2) % 8, (t + 4) % 8
    return [t, t ^ 1, a, b, c, a ^ 1, b ^ 1, c ^ 1]


def fill(at_ref, shards, fulls, sems):
    part = shards[0].shape[0]
    copies = []
    order = gather_order(at_ref[2])
    for i, s in enumerate(shards):
        at = pl.ds(pl.multiple_of(order[i % 8] * part, 16), part)
        copies.append(pltpu.make_async_copy(s, fulls[i // 8].at[at, :], sems[i // 8].at[i % 8]))
    for c in copies:
        c.start()
    for c in copies:
        c.wait()


def memory_kernel(at_ref, pick_ref, *refs):
    xs, ms = refs[:8], refs[8:16]
    w_ref, gain_ref, out_ref, x_ref, m_ref, rows_ref, x_sems, m_sems = refs[16:]
    fill(at_ref, xs + ms, (x_ref, m_ref), (x_sems, m_sems))
    half = w_ref.shape[0] // 4
    mine = pl.ds(pl.multiple_of(at_ref[0] * half, 128), half)
    rest = pl.ds(pl.multiple_of((1 - at_ref[0]) * half, 128), half)
    kv = jnp.zeros((2 * HD, rows_ref.shape[0]), F32)
    for i, rows in enumerate((x_ref[mine, :], m_ref[mine, :], x_ref[rest, :], m_ref[rest, :])):
        kv += dot(w_ref[i * half : (i + 1) * half], rows, ((0,), (0,)))
    keys = kv[:HD]
    keys = keys * lax.rsqrt(jnp.mean(keys * keys, 0, keepdims=True) + 1e-05) * gain_ref[...]
    rows_ref[:, :HD] = jnp.transpose(keys).astype(BF)
    rows_ref[:, HD:] = jnp.transpose(kv[HD:]).astype(BF)
    for i in range(out_ref.shape[0] // 64):
        at = pl.ds(pl.multiple_of(pick_ref[i] * 64, 64), 64)
        out_ref[i * 64 : (i + 1) * 64, :] = rows_ref[at, :]


def finish(score_ref, mixed_ref, valid, out_ref):
    rows = out_ref.shape[1]
    scores = jnp.where(valid, score_ref[...] * HD ** (-0.5), -1e30)
    weights = jnp.exp(scores - jnp.max(scores, 1, keepdims=True))
    return (weights / jnp.sum(weights, 1, keepdims=True)).astype(BF)


def spread(mixed_ref, out_ref):
    group = out_ref.shape[2] // HD
    for s in range(STEPS):
        for h in range(group):
            out_ref[s, :, h * HD : (h + 1) * HD] = mixed_ref[:, s * group + h, :].astype(BF)


def cross_kernel(slot_ref, pipe_ref, count_ref, q_ref, own_ref, other_ref, out_ref, score_ref, prob_ref, mixed_ref):
    rows, per = q_ref.shape[0], q_ref.shape[1]
    pipe = pipe_ref[0]
    for b in range(rows):
        at = pl.ds(pl.multiple_of(slot_ref[b] * 64, 64), 64)
        keys = jnp.concatenate([own_ref[at, :HD], other_ref[at, :HD]], 0)
        score_ref[b * per : (b + 1) * per, :] = dot(q_ref[b], keys, ((1,), (1,)))
    lane = lax.broadcasted_iota(jnp.int32, (1, 128), 1)
    tile = 2 * jnp.where(lane >= 64, 1 - pipe, pipe) + (lane % 64) // TT
    prob_ref[...] = finish(score_ref, mixed_ref, tile < count_ref[...], out_ref)
    for b in range(rows):
        at = pl.ds(pl.multiple_of(slot_ref[b] * 64, 64), 64)
        values = jnp.concatenate([own_ref[at, HD:], other_ref[at, HD:]], 0)
        mixed_ref[b] = jnp.dot(
            prob_ref[b * per : (b + 1) * per, :], values, preferred_element_type=F32
        )
    spread(mixed_ref, out_ref)


def self_kernel(len_ref, q_ref, kv_ref, out_ref, score_ref, prob_ref, mixed_ref):
    rows, per = q_ref.shape[0], q_ref.shape[1]
    for b in range(rows):
        score_ref[b * per : (b + 1) * per, :] = dot(q_ref[b], kv_ref[b, :, :HD], ((1,), (1,)))
    spots = kv_ref.shape[1]
    lane = lax.broadcasted_iota(jnp.int32, (1, spots), 1)
    step = (lax.broadcasted_iota(jnp.int32, (rows * per, 1), 0) % per) // (per // STEPS)
    valid = (lane < len_ref[...]) | ((lane >= LMAX) & (lane <= LMAX + step))
    prob_ref[...] = finish(score_ref, mixed_ref, valid, out_ref)
    for b in range(rows):
        mixed_ref[b] = jnp.dot(
            prob_ref[b * per : (b + 1) * per, :], kv_ref[b, :, HD:], preferred_element_type=F32
        )
    spread(mixed_ref, out_ref)


ZX = [(t, t ^ 1) for t in range(8)]


def y_perm(d):
    return [(t, (t + 2 * d) % 8) for t in range(8)]


def gather8(s, near, hold):
    p1, p2, p3 = y_perm(1), y_perm(2), y_perm(3)
    z = lax.ppermute(s, "tensor", ZX)
    a, b, c = (lax.ppermute(near, "tensor", p) for p in (p1, p3, p2))
    z = after(z, *hold(a, b, c))
    za, zb, zc = (lax.ppermute(z, "tensor", p) for p in (p1, p3, p2))
    return (s, z, a, b, c, za, zb, zc)


def after(value, *others):
    return lax.optimization_barrier((value,) + others)[0]


def swap(values, axis, bit, size):
    return lax.ppermute(values, axis, [(i, i ^ bit) for i in range(size)])


def choose(flag, a, b):
    return jnp.where(flag, a, b)


def out_rows(enc_out_w, replica, pipe):
    per = ENC_W // 32
    pairs = []
    for r in range(16):
        for p in range(2):
            for t in range(8):
                part = p * 4 + r // 4
                near = t % 2 == part % 2
                source = t // 2 * 4 + (r % 4 if near else 3 - r % 4)
                core = 0 if near else 1
                pairs.append(((source * 2 + core) * 8 + part, (r * 2 + p) * 8 + t))
    block = jnp.where(pipe == 0, replica % 4, 3 - replica % 4)
    mine = lax.dynamic_slice_in_dim(enc_out_w, block * per, per)
    return lax.ppermute(mine, ("replica", "pipe", "tensor"), pairs)


def heads_kernel(part_ref, out_ref):
    for h in range(KV_HEADS):
        out_ref[h, :, :HD] = part_ref[0, :, h * HD : (h + 1) * HD]
        out_ref[h, :, HD:] = part_ref[1, :, h * HD : (h + 1) * HD]


def fold_weights(few, proj_w, cross_kv_w, replica, pipe):
    per = ENC_W // 32
    folded = jnp.dot(few, proj_w, preferred_element_type=F32).astype(BF)
    left = lax.dynamic_slice_in_dim(proj_w, (pipe * 16 + replica) * per, per)
    left = jnp.concatenate([left, folded], 0)
    part = jnp.einsum("rk,kcn->crn", left, cross_kv_w, preferred_element_type=F32).astype(BF)
    return call(
        heads_kernel,
        shape_of((KV_HEADS, 2 * per, 2 * HD), BF),
        [VMEM],
        [],
        0,
        2 * part.size * 2,
        "heads",
    )(part)


def line_shift(d):
    return [(r, r // 4 * 4 + (r + d) % 4) for r in range(16)]


def plane_shift(d):
    return [(r, (r + 4 * d) % 16) for r in range(16)]


def ring_of(piece, shift):
    return jnp.stack([piece] + [lax.ppermute(piece, "replica", shift(d)) for d in (1, 2, 3)])


def shards(
    patches,
    tile_counts,
    ln_gain,
    enc_qkv,
    enc_out_w,
    proj_w,
    cross_kv_w,
    k_gain,
    plan,
    row_pick,
    q_cross,
    q_self,
    cache_kv,
    new_kv,
    kv_len,
):
    replicas = 16
    group = lax.axis_index("replica")
    pipe = lax.axis_index("pipe")
    tensor = lax.axis_index("tensor")
    images, held, tile_rows, part = patches.shape
    rows = images * held * tile_rows
    pipe_at = jnp.stack([pipe, group, tensor]).astype(jnp.int32)

    turned = call(
        turn_kernel, shape_of((part, rows), BF), [VMEM], [], 2 * rows * part * part, 4 * rows * part, "turn"
    )(patches.reshape(rows, part))
    few = out_rows(enc_out_w, group, pipe)
    blocks = fold_weights(few, proj_w, cross_kv_w, group, pipe)
    norm_gain = ln_gain.reshape(ENC_W, 1)
    xs = gather8(turned, after(turned, few, norm_gain), lambda *_: (blocks,))

    turned_w = enc_qkv.transpose(1, 2, 0).reshape(3 * part, ENC_W)
    q, kv = call(
        qkv_kernel,
        (shape_of((part, rows), BF), shape_of((2 * part, rows), BF)),
        [SMEM] + [ANY] * 10,
        [
            pltpu.VMEM((ENC_W, rows), BF),
            pltpu.VMEM((3 * part, ENC_W), BF),
            pltpu.VMEM((ENC_W, 1), F32),
            pltpu.SemaphoreType.DMA((8,)),
            pltpu.SemaphoreType.DMA((2,)),
        ],
        2 * rows * ENC_W * 3 * part,
        6 * 1024 * 1024,
        "qkv",
    )(pipe_at, *xs, turned_w, norm_gain)
    kv_other = lax.ppermute(kv, "pipe", [(0, 1), (1, 0)])
    mixed = call(
        attend_kernel,
        shape_of((part, rows), BF),
        [SMEM, SMEM, VMEM, VMEM, VMEM],
        [],
        4 * rows * 256 * part,
        2 * 1024 * 1024,
        "encoder_attend",
    )(tile_counts, pipe_at, q, kv, kv_other)

    parts = lax.all_to_all(blocks, "tensor", split_axis=0, concat_axis=0, tiled=True)
    piece = jnp.sum(after(parts, kv).astype(F32), 0).astype(BF)
    line = ring_of(piece, line_shift)
    ms = gather8(mixed, mixed, lambda *abc: abc)
    line = after(line, mixed)
    line_other = lax.ppermute(line, "pipe", [(0, 1), (1, 0)])
    plane = ring_of(after(jnp.stack([line, line_other]), mixed), plane_shift)
    spot = jnp.arange(16)
    spot = (group // 4 - spot // 4) % 4 * 4 + (group - spot) % 4
    plane = jnp.moveaxis(plane, 1, 0).reshape(2, 16, 2, -1, 2 * HD)
    pieces = jnp.moveaxis(jnp.take(plane, spot, axis=1), 2, 1).reshape(2 * ENC_W, 2 * HD)

    destination = after(plan, ms[1])[:, 0]
    grouped = destination.reshape(replicas, images)
    earlier = jnp.arange(images)[:, None] < jnp.arange(images)[None, :]
    same_dest = grouped[:, :, None] == grouped[:, None, :]
    ranks = jnp.sum((same_dest & earlier[None]).astype(jnp.int32), 1)
    my_dest = lax.dynamic_index_in_dim(grouped, group, 0, keepdims=False)
    my_rank = lax.dynamic_index_in_dim(ranks, group, 0, keepdims=False)
    spot = my_dest * CAP + my_rank
    picks = jnp.sum(
        jnp.where(
            spot[None, :] == jnp.arange(replicas * CAP)[:, None],
            jnp.arange(images, dtype=jnp.int32)[None, :],
            0,
        ),
        1,
    ).astype(jnp.int32)
    mine = (destination == group).astype(jnp.int32)
    count = jnp.sum(mine)
    before = jnp.cumsum(mine) - mine
    wanted = row_pick % count
    hit = (mine[None, :] == 1) & (before[None, :] == wanted[:, None])
    every = jnp.arange(replicas * images, dtype=jnp.int32)
    slot_of = (every // images) * CAP + ranks.reshape(-1)
    slot_ids = jnp.sum(jnp.where(hit, slot_of[None, :], 0), 1).astype(jnp.int32)
    counts_rows = jnp.sum(jnp.where(hit, tile_counts[None, :], 0), 1).astype(jnp.int32)
    gain = k_gain.reshape(HD, 1)
    slots = call(
        memory_kernel,
        shape_of((replicas * CAP * held * tile_rows, 2 * HD), BF),
        [SMEM] * 2 + [ANY] * 16 + [VMEM] * 2,
        [
            pltpu.VMEM((ENC_W, rows), BF),
            pltpu.VMEM((ENC_W, rows), BF),
            pltpu.VMEM((rows, 2 * HD), BF),
            pltpu.SemaphoreType.DMA((8,)),
            pltpu.SemaphoreType.DMA((8,)),
        ],
        4 * rows * ENC_W * 2 * HD,
        6 * 1024 * 1024,
        "memory",
    )(pipe_at, picks, *xs, *ms, pieces, gain)
    arrived = lax.all_to_all(slots, "replica", split_axis=0, concat_axis=0, tiled=True)
    q_self, q_cross, cache_kv, new_kv, kv_len = (after(v, slots) for v in (q_self, q_cross, cache_kv, new_kv, kv_len))
    rows_here = row_pick.shape[0]
    steps_heads = q_self.shape[0] * q_self.shape[2] // HD

    def heads_of(q):
        return q.reshape(STEPS, rows_here, -1, HD).transpose(1, 0, 2, 3).reshape(rows_here, steps_heads, HD)

    spots = 48
    joined = jnp.concatenate(
        [
            cache_kv.reshape(rows_here, LMAX, 2 * HD),
            jnp.moveaxis(new_kv, 0, 1).reshape(rows_here, STEPS, 2 * HD),
            jnp.zeros((rows_here, spots - LMAX - STEPS, 2 * HD), BF),
        ],
        1,
    )

    def per_head(values):
        return jnp.repeat(values.astype(jnp.int32), steps_heads).reshape(rows_here * steps_heads, 1)

    def scratch(n):
        return [
            pltpu.VMEM((rows_here * steps_heads, n), F32),
            pltpu.VMEM((rows_here * steps_heads, n), BF),
            pltpu.VMEM((rows_here, steps_heads, HD), F32),
        ]

    self_out = call(
        self_kernel,
        shape_of(q_self.shape, BF),
        [VMEM] * 3,
        scratch(spots),
        4 * rows_here * 16 * 128 * 128,
        4 * 1024 * 1024,
        "self_attend",
    )(per_head(kv_len), heads_of(q_self), joined)
    cross_heads, cross_counts = heads_of(q_cross), per_head(counts_rows)
    arrived = after(arrived, self_out, cross_heads, cross_counts, slot_ids)
    arrived_other = lax.ppermute(arrived, "pipe", [(0, 1), (1, 0)])

    cross_out = call(
        cross_kernel,
        shape_of(q_cross.shape, BF),
        [SMEM, SMEM] + [VMEM] * 4,
        scratch(128),
        4 * rows_here * 16 * 128 * 128,
        4 * 1024 * 1024,
        "cross_attend",
    )(slot_ids, pipe_at, cross_counts, cross_heads, arrived, arrived_other)
    return (cross_out, self_out)


def solution(mesh):
    in_specs = (
        P("replica", "pipe", None, "tensor"),
        P(),
        P(),
        P(None, None, "tensor"),
        P("tensor", None),
        P(None, "tensor"),
        P("tensor", None, None),
        P(),
        P(),
        P(("replica", "pipe")),
        P(None, ("replica", "pipe"), "tensor"),
        P(None, ("replica", "pipe"), "tensor"),
        P(("replica", "pipe"), None, None, "tensor"),
        P(None, ("replica", "pipe"), None, "tensor"),
        P(("replica", "pipe")),
    )
    out_specs = (P(None, ("replica", "pipe"), "tensor"), P(None, ("replica", "pipe"), "tensor"))
    return jax.shard_map(shards, mesh=mesh, in_specs=in_specs, out_specs=out_specs, check_vma=False)
```
